32 devices in a mesh: dp: 16 (over z, y, x), mp: 2 (over core).
Axes of the slice: x: 2, y: 2, z: 4, core: 2. Of those that a mesh axis runs over, the one named last changes fastest.
Arguments:
- inputs: bfloat16 [2, 16, 256, 2048], P(None, 'dp'), may hold values from -6 to 6
- segment_ids: int32 [2, 16, 256], P(None, 'dp'), may hold values from 0 to 3, never falling along the last dimension, each value on 1 to 128 neighbouring positions
- cotangent: bfloat16 [2, 16, 256, 2048], P(None, 'dp'), may hold values from -6 to 6
- mixer_gain: bfloat16 [2048], P('dp'), may hold values from 0.5 to 1.5
- mlp_gain: bfloat16 [2048], P('dp'), may hold values from 0.5 to 1.5
- w_branch: bfloat16 [2048, 2560], P('dp', 'mp'), may hold values from -0.125 to 0.125
- w_recur: bfloat16 [2048, 2560], P('dp', 'mp'), may hold values from -0.125 to 0.125
- conv_w: bfloat16 [4, 2560], P(None, ('mp', 'dp')), may hold values from -3 to 3
- w_decay: bfloat16 [16, 25600], P('mp', 'dp'), may hold values from -0.5 to 0.5
- w_input: bfloat16 [16, 25600], P('mp', 'dp'), may hold values from -0.5 to 0.5
- gate_bias: bfloat16 [2, 2560], P(None, ('mp', 'dp')), may hold values from -4 to 4
- decay_param: bfloat16 [2560], P(('mp', 'dp')), may hold values from 1.5 to 6
- w_out: bfloat16 [2560, 2048], P('mp', 'dp'), may hold values from -0.3125 to 0.3125
- w_gate: bfloat16 [2048, 6144], P('dp', 'mp'), may hold values from -0.125 to 0.125
- w_up: bfloat16 [2048, 6144], P('dp', 'mp'), may hold values from -0.125 to 0.125
- w_down: bfloat16 [6144, 2048], P('mp', 'dp'), may hold values from -0.15625 to 0.15625
Outputs:
- result: float32 [2, 16, 256, 2048], P(None, 'dp')
- input_grad: float32 [2, 16, 256, 2048], P(None, 'dp')
- grad_mixer_gain: float32 [2048], P('dp')
- grad_mlp_gain: float32 [2048], P('dp')
- grad_w_branch: float32 [2048, 2560], P('dp', 'mp')
- grad_w_recur: float32 [2048, 2560], P('dp', 'mp')
- grad_conv_w: float32 [4, 2560], P(None, ('mp', 'dp'))
- grad_w_decay: float32 [16, 25600], P('mp', 'dp')
- grad_w_input: float32 [16, 25600], P('mp', 'dp')
- grad_gate_bias: float32 [2, 2560], P(None, ('mp', 'dp'))
- grad_decay_param: float32 [2560], P(('mp', 'dp'))
- grad_w_out: float32 [2560, 2048], P('mp', 'dp')
- grad_w_gate: float32 [2048, 6144], P('dp', 'mp')
- grad_w_up: float32 [2048, 6144], P('dp', 'mp')
- grad_w_down: float32 [6144, 2048], P('mp', 'dp')
The draws below stay inside these ranges and needn't reach their ends.
Inputs may be any that keep to these rules, and one draw needn't show every extreme that they name: `segment_ids`: along each row the ids never fall; a segment spans 1 to 128 positions.
All inputs are finite; a program needn't handle non-finite values.
Results may differ from the reference program's by a relative error of at most 0.01.
Values may be sent and summed in bfloat16 or wider, within the bound.
No kernel may reach another device: no remote copies, remote signals or barrier semaphores. Data moves between devices by JAX's collectives and lax.ppermute only.
A program may use at most 320 MiB of HBM per device.

```python
import math
import jax
import jax.numpy as jnp
import numpy as np
from jax import lax

D = 2048
RNN = 2560
HEADS = 16
BW = 160
FF = 6144
CONV = 4
ROW = 256
MICRO = 2
BATCH = 16


def raised(drawn, rng, source, target, parts, factor):
    def block_of(position):
        return (jnp.arange(drawn.shape[position]) // (drawn.shape[position] // parts)).reshape((-1,) + (1,) * (drawn.ndim - 1 - position))

    one_side = jax.random.permutation(rng, parts)[block_of(target)]
    other_side = (block_of(target) + parts // 2) % parts
    return jnp.where((block_of(source) == one_side) | (block_of(source) == other_side), factor * drawn, drawn)


def block_scale(rng, shape, cuts, smallest, top_value):
    level = 1.0
    for axis_at, parts in cuts:
        draws = jax.random.uniform(jax.random.fold_in(jax.random.fold_in(rng, 6), axis_at), (parts,), jnp.float32, smallest / len(cuts), top_value / len(cuts))
        level = level * jnp.repeat(jnp.exp(draws), shape[axis_at] // parts).reshape((-1,) + (1,) * (len(shape) - 1 - axis_at))
    return level


def split_up(amount, total, most, skew):
    loads = [(1 << 20) // math.isqrt(rank ** skew) + 1 for rank in range(2, amount + 1)]
    rest, counts = total - most - (amount - 1), [1] * (amount - 1)
    while rest > 0:
        free = [i for i in range(amount - 1) if counts[i] < most]
        whole, budget = sum([loads[i] for i in free]), rest
        for i in free:
            more = min(most - counts[i], max(1, budget * loads[i] // whole), rest)
            counts[i] = counts[i] + more
            rest = rest - more
    return np.array([most] + counts)


def ragged_sizes(own_key, count, total, bound, lean):
    if count == 2:
        one = jax.random.randint(own_key, (), max(1, total - bound), min(bound, total - 1) + 1)
        return jnp.stack([one, total - one])
    sizes = jnp.asarray(split_up(count, total, bound, lean), jnp.int32)
    twos = (count - 1) // 2
    giver, taker = sizes[1:1 + 2 * twos:2], sizes[2:2 + 2 * twos:2]
    margin = jnp.minimum(giver - 1, bound - taker)
    moved = jax.random.randint(jax.random.fold_in(own_key, 1), (twos,), 0, 1 << 20) % (margin + 1)
    sizes = sizes.at[1:1 + 2 * twos:2].set(giver - moved).at[2:2 + 2 * twos:2].set(taker + moved)
    return sizes[jax.random.permutation(jax.random.fold_in(own_key, 2), count)]


def gaussian(own_key, dims, deviation, bound, cuts=(), kind=jnp.bfloat16):
    result = jax.random.normal(own_key, dims, jnp.float32) * deviation
    if len(cuts) > 0:
        result = block_scale(own_key, dims, cuts, -0.22, 0.18) * result
    return jnp.clip(result, min=-bound, max=bound).astype(kind)


def gaussian_with(rng, dims, scale, limit, cuts, heavy, kind=jnp.bfloat16):
    values = scale * jax.random.normal(rng, dims, jnp.float32)
    if cuts:
        values = values * block_scale(rng, dims, cuts, -0.22, 0.18)
    return jnp.clip(raised(values, jax.random.fold_in(rng, 3), *heavy), -limit, limit).astype(kind)


def setup_inputs(seed: int = 0) -> dict:
    key_list = jax.random.split(jax.random.key(seed), 17)
    inputs = gaussian_with(key_list[0], (MICRO, BATCH, ROW, D), 1.0, 6.0, ((1, 16),), (1, 3, 16, 2.0))
    segment_ids = jax.vmap(lambda own: jnp.searchsorted(jnp.cumsum(ragged_sizes(own, 4, ROW, ROW // 2, 0)), jnp.arange(ROW), side="right"))(jax.random.split(key_list[1], MICRO * BATCH)).reshape((MICRO, BATCH, ROW)).astype(jnp.int32)
    cotangent = gaussian_with(key_list[2], (MICRO, BATCH, ROW, D), 1.0, 6.0, ((1, 16),), (1, 3, 16, 2.0))
    mixer_gain = jnp.clip(1.0 + 0.1 * jax.random.normal(key_list[3], (D,), jnp.float32), 0.5, 1.5).astype(jnp.bfloat16)
    mlp_gain = jnp.clip(1.0 + 0.1 * jax.random.normal(key_list[4], (D,), jnp.float32), 0.5, 1.5).astype(jnp.bfloat16)
    w_branch = gaussian(key_list[5], (D, RNN), D ** -0.5, 0.125, ((0, 16), (1, 2)))
    w_recur = gaussian(key_list[6], (D, RNN), D ** -0.5, 0.125, ((0, 16), (1, 2)))
    conv_w = gaussian(key_list[7], (CONV, RNN), CONV ** -0.5, 3.0, ((1, 32),))
    w_decay = gaussian(key_list[8], (HEADS, BW * BW), BW ** -0.5, 0.5, ((0, 2), (1, 16)))
    w_input = gaussian(key_list[9], (HEADS, BW * BW), BW ** -0.5, 0.5, ((0, 2), (1, 16)))
    gate_bias = gaussian(key_list[10], (2, RNN), 1.0, 4.0, ((1, 32),))
    decay_param = jnp.clip(1.5 + 4.5 * jax.random.uniform(key_list[11], (RNN,), jnp.float32) ** block_scale(key_list[11], (RNN,), ((0, 32),), -0.2, 0.2), 1.5, 6.0).astype(jnp.bfloat16)
    w_out = gaussian(key_list[12], (RNN, D), (RNN // 8) ** -0.5, 0.3125, ((0, 2), (1, 16)))
    w_gate = gaussian(key_list[13], (D, FF), D ** -0.5, 0.125, ((0, 16), (1, 2)))
    w_up = gaussian(key_list[14], (D, FF), D ** -0.5, 0.125, ((0, 16), (1, 2)))
    w_down = gaussian(key_list[15], (FF, D), (FF // 4) ** -0.5, 0.15625, ((0, 2), (1, 16)))
    return dict(inputs=inputs, segment_ids=segment_ids, cotangent=cotangent, mixer_gain=mixer_gain, mlp_gain=mlp_gain, w_branch=w_branch, w_recur=w_recur, conv_w=conv_w, w_decay=w_decay, w_input=w_input, gate_bias=gate_bias, decay_param=decay_param, w_out=w_out, w_gate=w_gate, w_up=w_up, w_down=w_down)


@jax.custom_vjp
def low(v):
    return lax.optimization_barrier(v.astype(jnp.bfloat16)).astype(jnp.float32)

@jax.custom_vjp
def low_back(v):
    return v

def low_keep(v):
    return (low(v), None)

def low_pass(kept, grad):
    return (grad,)

def back_keep(v):
    return (v, None)

def back_low(kept, grad):
    return (low(grad),)
low.defvjp(low_keep, low_pass)
low_back.defvjp(back_keep, back_low)

def matmul(left_in, right_in):
    return jnp.dot(left_in, right_in, precision=lax.Precision.HIGHEST)

def rms_scale(values, norm_gain):
    return values * lax.rsqrt(lax.optimization_barrier(jnp.mean(values * values, axis=-1, keepdims=True)) + 1e-06) * norm_gain

def same_masks(seg_rows, tap_count):
    same_seg = []
    for offset in range(1, tap_count):
        matched = (seg_rows[..., offset:] == seg_rows[..., :-offset]).astype(jnp.float32)
        leading = jnp.zeros(seg_rows.shape[:-1] + (offset,), jnp.float32)
        same_seg.append(jnp.concatenate([leading, matched], axis=-1)[..., None])
    return same_seg

def conv_mix(signal, conv_f, same_seg):
    summed = signal * conv_f[0]
    for offset in range(1, conv_f.shape[0]):
        widths = [(0, 0)] * (signal.ndim - 2) + [(offset, 0), (0, 0)]
        shifted = jnp.pad(signal, widths)[..., :-offset, :]
        summed = summed + conv_f[offset] * shifted * same_seg[offset - 1]
    return summed

def combine(earlier, latest):
    return (earlier[0] * latest[0], latest[0] * earlier[1] + latest[1])

def recur(branch, decay_pre, input_pre, values, biases, raw_decay, resets):
    r_gate = jax.nn.sigmoid(decay_pre + biases[0])
    i_gate = jax.nn.sigmoid(input_pre + biases[1])
    log_decay = -8.0 * r_gate * jax.nn.softplus(-raw_decay)
    carry_on = 1.0 - resets
    norm_mult = resets + carry_on * jnp.sqrt(-jnp.expm1(2.0 * log_decay))
    decay_now = jnp.exp(log_decay) * carry_on
    drive_in = norm_mult * i_gate * values
    _, hidden = lax.associative_scan(combine, (decay_now, drive_in), axis=values.ndim - 2)
    return hidden * jax.nn.gelu(branch)

def head_mix(heads_view, weights):
    width = heads_view.shape[-1]
    blocks = weights.reshape(weights.shape[0], width, width)
    return jnp.einsum('grhc,hcd->grhd', heads_view, blocks, precision=lax.Precision.HIGHEST)

def forward(params, x_float, seg_rows):
    mixer_gain, mlp_gain, w_branch, w_recur, conv_w, w_decay, w_input, gate_bias, decay_param, w_out, w_gate, w_up, w_down = params
    same_seg = same_masks(seg_rows, conv_w.shape[0])
    resets = 1.0 - same_seg[0]
    normed_mix = low(rms_scale(x_float, mixer_gain))
    branch = low_back(matmul(normed_mix, w_branch))
    recur_in = low_back(matmul(normed_mix, w_recur))
    values = low(conv_mix(recur_in, conv_w, same_seg))
    heads_view = values.reshape(values.shape[:-1] + (HEADS, RNN // HEADS))
    decay_pre = low_back(head_mix(heads_view, w_decay)).reshape(values.shape)
    input_pre = low_back(head_mix(heads_view, w_input)).reshape(values.shape)
    mixed = low(recur(branch, decay_pre, input_pre, values, gate_bias, decay_param, resets))
    after_mix = x_float + low_back(matmul(mixed, w_out))
    normed_mlp = low(rms_scale(after_mix, mlp_gain))
    gate_pre = low_back(matmul(normed_mlp, w_gate))
    up_pre = low_back(matmul(normed_mlp, w_up))
    hidden = low(jax.nn.gelu(gate_pre) * up_pre)
    return after_mix + low_back(matmul(hidden, w_down))

def reference(inputs, segment_ids, cotangent, mixer_gain, mlp_gain, w_branch, w_recur, conv_w, w_decay, w_input, gate_bias, decay_param, w_out, w_gate, w_up, w_down):
    params = tuple((p.astype(jnp.float32) for p in (mixer_gain, mlp_gain, w_branch, w_recur, conv_w, w_decay, w_input, gate_bias, decay_param, w_out, w_gate, w_up, w_down)))
    row_count = MICRO * BATCH
    group = math.gcd(row_count, max(1, 4096 // ROW))
    blocks = row_count // group
    x_blocks = inputs.reshape(blocks, group, ROW, D).astype(jnp.float32)
    seg_blocks = segment_ids.reshape(blocks, group, ROW).astype(jnp.int32)
    cot_blocks = cotangent.reshape(blocks, group, ROW, D).astype(jnp.float32)

    def one_block(summed, pieces):
        x_block, seg_block, cot_block = pieces

        def apply_block(x_value, weights):
            return forward(weights, x_value, seg_block)
        outcome, pull_back = jax.vjp(apply_block, x_block, params)
        x_grad, weight_grads = pull_back(cot_block)
        summed = jax.tree.map(lambda left_in, right_in: left_in + right_in, summed, weight_grads)
        return (summed, (outcome, x_grad))
    start = tuple((jnp.zeros_like(p) for p in params))
    summed, (outcome, x_grad) = lax.scan(one_block, start, (x_blocks, seg_blocks, cot_blocks))
    return (outcome.reshape(MICRO, BATCH, ROW, D), x_grad.reshape(MICRO, BATCH, ROW, D), summed[0], summed[1], summed[2], summed[3], summed[4], summed[5], summed[6], summed[7], summed[8], summed[9], summed[10], summed[11], summed[12])
```

```python
import functools

import jax
import jax.numpy as jnp
from jax import lax
from jax.experimental import pallas as pl
from jax.experimental.pallas import tpu as pltpu
from jax.sharding import PartitionSpec as P

BW = 160
G = 4
BF = jnp.bfloat16
F32 = jnp.float32
ROWS = 8
PAD = 8
C0 = 0.7978845608028654
C1 = 0.044715


def sigmoid(v):
    return 0.5 * jnp.tanh(0.5 * v) + 0.5


def gates(dec, inp, sp8, keep):
    r = sigmoid(dec)
    i = sigmoid(inp)
    log_decay = r * sp8
    a = jnp.exp(log_decay)
    gap = -jnp.tanh(log_decay) * (1.0 + a * a)
    return r, i, a, gap


def forward_kernel(cp, row, unroll, mix_hbm, mask_ref, par_ref, wg_ref, mixed_ref, values_ref, pre_ref, h_ref, vals, mixf, mix, sems):
    lanes = cp // 128
    order = list(range(lanes, 2 * lanes)) + list(range(lanes))
    copies = {
        j: [pltpu.make_async_copy(mix_hbm.at[pl.ds(r * row, row), pl.ds(128 * j, 128)], mix.at[j, pl.ds(r * (row + PAD), row)], sems.at[j, r]) for r in range(ROWS)] for j in order
    }
    for j in order:
        for c in copies[j]:
            c.start()

    def at(ref, t, off=0):
        return [ref[off + j, pl.ds(t, ROWS, stride=row + PAD), :] for j in range(lanes)]

    def put(ref, t, tiles):
        for j in range(lanes):
            ref[j, pl.ds(t, ROWS, stride=row + PAD), :] = tiles[j]

    def flat(ref, rows):
        return jnp.concatenate([ref[j, rows, :] for j in range(lanes)], axis=1)

    def mask(k, t):
        return mask_ref[k, pl.ds(pl.multiple_of(t * ROWS, ROWS), ROWS), :]

    par = [[par_ref[p, :, pl.ds(128 * j, 128)] for j in range(lanes)] for p in range(7)]
    zero = [jnp.zeros((ROWS, 128), F32)] * lanes
    for j in order[:lanes]:
        for c in copies[j]:
            c.wait()

    def conv_step(blk, carry):
        prev = [list(carry[0:lanes]), list(carry[lanes:2 * lanes]), list(carry[2 * lanes:])]
        for u in range(unroll):
            t = blk * unroll + u
            now = at(mix, t, lanes)
            same = [mask(k, t) for k in range(3)]
            out = []
            for j in range(lanes):
                s = now[j] * par[0][j]
                for k in range(3):
                    s = s + par[k + 1][j] * prev[k][j] * same[k]
                out.append(s)
            put(vals, t, out)
            prev = [now, prev[0], prev[1]]
        return tuple(prev[0] + prev[1] + prev[2])

    lax.fori_loop(0, row // unroll, conv_step, tuple(zero * 3))

    for r in range(ROWS):
        rows = pl.ds(r * row, row)
        prow = pl.ds(r * (row + PAD), row)
        low = flat(vals, prow).astype(BF)
        values_ref[rows, :] = low
        pre = jnp.dot(low, wg_ref[...], preferred_element_type=F32)
        for j in range(2 * lanes):
            pre_ref[j, prow, :] = pre[:, 128 * j : 128 * (j + 1)]
    for j in order[lanes:]:
        for c in copies[j]:
            c.wait()

    def step(blk, carry):
        h = list(carry)
        for u in range(unroll):
            t = blk * unroll + u
            dec, inp, val, br = at(pre_ref, t), at(pre_ref, t, lanes), at(vals, t), at(mix, t)
            keep = mask(0, t)
            out = []
            for j in range(lanes):
                r, i, a, gap = gates(dec[j] + par[4][j], inp[j] + par[5][j], par[6][j], keep)
                m = (1.0 - keep) + keep * jnp.sqrt(jnp.maximum(gap, 0.0))
                v = val[j].astype(BF).astype(F32)
                h[j] = a * keep * h[j] + m * i * v
                b = br[j]
                tt = jnp.tanh(C0 * (b + C1 * b * b * b))
                out.append(h[j] * (0.5 * b * (1.0 + tt)))
            put(h_ref, t, h)
            put(mixf, t, out)
        return tuple(h)

    lax.fori_loop(0, row // unroll, step, tuple(zero))
    for r in range(ROWS):
        rows = pl.ds(r * row, row)
        mixed_ref[rows, :] = flat(mixf, pl.ds(r * (row + PAD), row)).astype(BF)


def forward_call(mix, mask, par, wg, unroll=8):
    tokens, cp = mix.shape[0], mix.shape[1] // 2
    row = tokens // ROWS
    lanes = cp // 128
    vm = pl.BlockSpec(memory_space=pltpu.VMEM)
    return pl.pallas_call(
        functools.partial(forward_kernel, cp, row, unroll),
        in_specs=[pl.BlockSpec(memory_space=pl.ANY), vm, vm, vm],
        out_specs=(vm, vm, vm, vm),
        out_shape=(
            jax.ShapeDtypeStruct((tokens, cp), BF),
            jax.ShapeDtypeStruct((tokens, cp), BF),
            jax.ShapeDtypeStruct((2 * lanes, tokens + ROWS * PAD, 128), F32),
            jax.ShapeDtypeStruct((lanes, tokens + ROWS * PAD, 128), F32),
        ),
        scratch_shapes=[
            pltpu.VMEM((lanes, tokens + ROWS * PAD, 128), F32),
            pltpu.VMEM((lanes, tokens + ROWS * PAD, 128), F32),
            pltpu.VMEM((2 * lanes, tokens + ROWS * PAD, 128), F32),
            pltpu.SemaphoreType.DMA((2 * lanes, ROWS)),
        ],
        compiler_params=pltpu.CompilerParams(vmem_limit_bytes=60 * 1024 * 1024),
        name="recur_forward",
    )(mix, mask, par, wg)


def backward_kernel(
    cp, row, unroll, mix_hbm, gm_hbm, mask_ref, par_ref, wg_ref, values_ref, pre_ref, h_ref,
    mixlow_ref, low_ref, acc_ref, vals, mix, gm, gdec, ginp, gval, sems,
):
    lanes = cp // 128
    pitch = row + PAD
    copies = []
    for j in range(lanes):
        for r in range(ROWS):
            src = pl.ds(r * row, row)
            dst = pl.ds(r * pitch, row)
            cols = pl.ds(128 * j, 128)
            rec = pl.ds(cp + 128 * j, 128)
            copies.append(pltpu.make_async_copy(mix_hbm.at[src, cols], mix.at[j, dst], sems.at[0, j, r]))
            copies.append(
                pltpu.make_async_copy(mix_hbm.at[src, rec], mix.at[lanes + j, dst], sems.at[1, j, r])
            )
            copies.append(pltpu.make_async_copy(gm_hbm.at[src, cols], gm.at[j, dst], sems.at[2, j, r]))
    for c in copies:
        c.start()

    def at(ref, t, off=0):
        return [ref[off + j, pl.ds(t, ROWS, stride=pitch), :] for j in range(lanes)]

    def put(ref, t, tiles):
        for j in range(lanes):
            ref[j, pl.ds(t, ROWS, stride=pitch), :] = tiles[j]

    def flat(ref, rows):
        return jnp.concatenate([ref[j, rows, :] for j in range(lanes)], axis=1)

    def mask(k, t):
        return mask_ref[k, pl.ds(pl.multiple_of(t * ROWS, ROWS), ROWS), :]

    par = [[par_ref[p, :, pl.ds(128 * j, 128)] for j in range(lanes)] for p in range(7)]
    zero = [jnp.zeros((ROWS, 128), F32)] * lanes
    for r in range(ROWS):
        low = values_ref[pl.ds(r * row, row), :].astype(F32)
        for j in range(lanes):
            vals[j, pl.ds(r * pitch, row), :] = low[:, 128 * j : 128 * (j + 1)]
    for c in copies:
        c.wait()

    def step(blk, carry):
        carry = [list(carry[lanes * p : lanes * (p + 1)]) for p in range(4)]
        ag, sum_dec, sum_inp, sum_raw = carry
        for u in range(unroll):
            t = row - 1 - (blk * unroll + u)
            dec, inp, val = at(pre_ref, t), at(pre_ref, t, lanes), at(vals, t)
            br, up, here, before = at(mix, t), at(gm, t), at(h_ref, t), at(h_ref, jnp.maximum(t - 1, 0))
            keep = mask(0, t)
            out_b, out_d, out_i, out_v = [], [], [], []
            for j in range(lanes):
                r, i, a, gap = gates(dec[j] + par[4][j], inp[j] + par[5][j], par[6][j], keep)
                gap = jnp.maximum(gap, 1e-30)
                inv = lax.rsqrt(gap)
                m = (1.0 - keep) + keep * (gap * inv)
                b = br[j]
                sq = b * b
                tt = jnp.tanh(C0 * (b + C1 * b * sq))
                half = 0.5 * (1.0 + tt)
                slope = half + 0.5 * b * (1.0 - tt * tt) * (C0 + 3.0 * C0 * C1 * sq)
                g = up[j] * (b * half) + ag[j]
                gi = g * i
                decay = a * keep
                g_log = g * before[j] * decay - gi * val[j] * keep * (a * a * inv)
                ag[j] = decay * g
                gr = g_log * r
                g_dec = gr * par[6][j] * (1.0 - r)
                g_dir = gi * m
                g_inp = g_dir * val[j] * (1.0 - i)
                sum_raw[j] = sum_raw[j] + gr
                sum_dec[j] = sum_dec[j] + g_dec
                sum_inp[j] = sum_inp[j] + g_inp
                out_b.append(up[j] * here[j] * slope)
                out_d.append(g_dec)
                out_i.append(g_inp)
                out_v.append(g_dir)
            put(gm, t, out_b)
            put(gdec, t, out_d)
            put(ginp, t, out_i)
            put(gval, t, out_v)
        return tuple(ag + sum_dec + sum_inp + sum_raw)

    sums = lax.fori_loop(0, row // unroll, step, tuple(zero * 4))
    for p in range(3):
        for j in range(lanes):
            acc_ref[4 + p, :, pl.ds(128 * j, 128)] = sums[lanes * (p + 1) + j]

    for r in range(ROWS):
        rows = pl.ds(r * row, row)
        prow = pl.ds(r * pitch, row)
        low = jnp.concatenate([flat(gdec, prow), flat(ginp, prow)], axis=1).astype(BF)
        low_ref[rows, :] = low
        back = lax.dot_general(low, wg_ref[...], (((1,), (1,)), ((), ())), preferred_element_type=F32)
        for j in range(lanes):
            gval[j, prow, :] = gval[j, prow, :] + back[:, 128 * j : 128 * (j + 1)]
        mixlow_ref[rows, pl.ds(0, cp)] = flat(gm, prow).astype(BF)

    def conv_step(blk, carry):
        carry = [list(carry[lanes * p : lanes * (p + 1)]) for p in range(10)]
        late, sums = carry[:6], carry[6:]
        for u in range(unroll):
            t = row - 1 - (blk * unroll + u)
            now, rec = at(gval, t), at(mix, t, lanes)
            same = [mask(k, t) for k in range(3)]
            taps = [now, late[0], late[1], late[3]]
            out = []
            for j in range(lanes):
                s = par[0][j] * now[j]
                for k in range(1, 4):
                    s = s + par[k][j] * taps[k][j]
                out.append(s)
                for k in range(4):
                    sums[k][j] = sums[k][j] + rec[j] * taps[k][j]
            put(gdec, t, out)
            scaled = [[now[j] * same[k] for j in range(lanes)] for k in range(3)]
            late = [scaled[0], late[2], scaled[1], late[4], late[5], scaled[2]]
        return tuple(sum(late + sums, []))

    sums = lax.fori_loop(0, row // unroll, conv_step, tuple(zero * 10))
    for k in range(4):
        for j in range(lanes):
            acc_ref[k, :, pl.ds(128 * j, 128)] = sums[lanes * (6 + k) + j]
    for r in range(ROWS):
        mixlow_ref[pl.ds(r * row, row), pl.ds(cp, cp)] = flat(gdec, pl.ds(r * pitch, row)).astype(BF)


def backward_call(mix, gm, mask, par, wg, values, pre, h, unroll=4):
    tokens, cp = gm.shape
    row = tokens // ROWS
    lanes = cp // 128
    vm = pl.BlockSpec(memory_space=pltpu.VMEM)
    hbm = pl.BlockSpec(memory_space=pl.ANY)
    slab = pltpu.VMEM((lanes, tokens + ROWS * PAD, 128), F32)
    return pl.pallas_call(
        functools.partial(backward_kernel, cp, row, unroll),
        in_specs=[hbm, hbm, vm, vm, vm, vm, vm, vm],
        out_specs=(vm, vm, vm),
        out_shape=(
            jax.ShapeDtypeStruct((tokens, 2 * cp), BF),
            jax.ShapeDtypeStruct((tokens, 2 * cp), BF),
            jax.ShapeDtypeStruct((7, ROWS, cp), F32),
        ),
        scratch_shapes=[
            slab,
            pltpu.VMEM((2 * lanes, tokens + ROWS * PAD, 128), F32),
            slab,
            slab,
            slab,
            slab,
            pltpu.SemaphoreType.DMA((3, lanes, ROWS)),
        ],
        compiler_params=pltpu.CompilerParams(vmem_limit_bytes=60 * 1024 * 1024),
        name="recur_backward",
    )(mix, gm, mask, par, wg, values, pre, h)


def rms_scale(values, norm_gain):
    return values * lax.rsqrt(jnp.mean(values * values, axis=-1, keepdims=True) + 1e-06) * norm_gain


def same_masks(seg_rows, tap_count):
    same_seg = []
    for offset in range(1, tap_count):
        matched = (seg_rows[..., offset:] == seg_rows[..., :-offset]).astype(F32)
        leading = jnp.zeros(seg_rows.shape[:-1] + (offset,), F32)
        same_seg.append(jnp.concatenate([leading, matched], axis=-1))
    return jnp.stack(same_seg)


def dot(a, b, ca, cb, out=F32):
    return lax.dot_general(a, b, (((ca,), (cb,)), ((), ())), preferred_element_type=out)


def unxor(pieces, g):
    low, high = (g & 1) == 1, (g >> 1) == 1
    p0, p1, p2, p3 = pieces
    q0, q1 = jnp.where(low, p1, p0), jnp.where(low, p0, p1)
    q2, q3 = jnp.where(low, p3, p2), jnp.where(low, p2, p3)
    return [
        jnp.where(high, q2, q0),
        jnp.where(high, q3, q1),
        jnp.where(high, q0, q2),
        jnp.where(high, q1, q3),
    ]


def make_body(n, m):
    far = n // G
    z_groups = [[c + G * k for k in range(far)] for c in range(G)]
    flips = [[(i, i ^ d) for i in range(n)] for d in range(G)]
    cores = [(0, 1), (1, 0)]

    def flip(a, d):
        return lax.ppermute(a, "dp", flips[d])

    far_flips = [[(i, i ^ (G * k)) for i in range(n)] for k in range(far)]

    def far_flip(a, k):
        return lax.ppermute(a, "dp", far_flips[k])

    def pick(a, i):
        return lax.dynamic_index_in_dim(a, i, 0, keepdims=False)

    def gather_far(a, z):
        got = jnp.stack([a] + [far_flip(a, k) for k in range(1, far)])
        return jnp.stack([pick(got, z ^ j) for j in range(far)])

    def sum_far(a, z, low=lambda v: v):
        total = pick(a, z)
        for k in range(1, far):
            total = total + far_flip(low(pick(a, z ^ k)), k).astype(F32)
        return total

    def swap_core(a):
        return lax.ppermute(a, "mp", cores)

    def gather8(own):
        mine = jnp.concatenate([own] + [flip(own, d) for d in range(1, G)], axis=0)
        return jnp.concatenate([mine, swap_core(mine)], axis=0)

    def scatter8(make, own_rows):
        other = make(1).astype(BF)
        arrived = swap_core(other)
        mine = make(0) + arrived.astype(F32)
        pieces = [mine[d * own_rows : (d + 1) * own_rows] for d in range(G)]
        total = pieces[0]
        for d in range(1, G):
            total = total + flip(pieces[d].astype(BF), d).astype(F32)
        return total

    def body(
        inputs,
        segment_ids,
        cotangent,
        mixer_gain,
        mlp_gain,
        w_branch,
        w_recur,
        conv_w,
        w_decay,
        w_input,
        gate_bias,
        decay_param,
        w_out,
        w_gate,
        w_up,
        w_down,
    ):
        dp = lax.axis_index("dp")
        mp = lax.axis_index("mp")
        g = dp % G
        z = dp // G
        micro, _, row, width = inputs.shape
        depth = width // n
        ch = w_branch.shape[1] // G
        ff = w_gate.shape[1] // G
        heads = w_decay.shape[0] // G
        taps = conv_w.shape[0]

        def own_part(a):
            return lax.dynamic_index_in_dim(a, mp, 0, keepdims=False)[0]

        x_own = own_part(inputs)
        c_own = own_part(cotangent)
        x_all = gather8(x_own)
        seg_all = gather8(own_part(segment_ids)[:, None])[:, 0].reshape(2 * G, row)

        small = jnp.concatenate(
            [a.reshape(-1) for a in (mixer_gain, mlp_gain, conv_w, gate_bias, decay_param)]
        )
        small = jnp.stack(unxor([small] + [flip(small, d) for d in range(1, G)], g))
        small = gather_far(small, z).reshape(n, -1).astype(F32)
        part = conv_w.shape[1]
        mixer_gain_f = small[:, :depth].reshape(width)
        mlp_gain_f = small[:, depth : 2 * depth].reshape(width)
        chan = small[:, 2 * depth :].reshape(n, taps + 3, part)
        chan = jnp.transpose(chan, (1, 0, 2)).reshape(taps + 3, n * part)
        chan = lax.dynamic_slice_in_dim(chan, g * ch, ch, 1)
        wide = -(-ch // 128) * 128
        sp8 = -8.0 * jax.nn.softplus(-chan[taps + 2 :])
        par = jnp.concatenate([chan[: taps + 2], sp8], axis=0)
        par = jnp.pad(par, ((0, 0), (0, wide - ch)), constant_values=((0, 0), (0, -1.0)))
        par = par * jnp.where((jnp.arange(wide) >= ch) & (jnp.arange(taps + 3) < taps + 2)[:, None], 0.0, 1.0)
        par_f = jnp.broadcast_to(par[:, None], (taps + 3, ROWS, wide))
        mask = jnp.transpose(same_masks(seg_all, taps), (0, 2, 1)).reshape(taps - 1, ROWS * row, 1)
        mask = jnp.broadcast_to(mask, (taps - 1, ROWS * row, 128))

        def fetch(weights):
            cols = [jnp.split(w, G, axis=1) for w in weights]
            blocks = [jnp.concatenate([c[j] for c in cols], axis=1) for j in range(G)]
            sends = unxor(blocks, g)
            got = [sends[0]] + [flip(sends[d], d) for d in range(1, G)]
            rows = jnp.concatenate(unxor(got, g), axis=0)
            return lax.all_gather(rows, "dp", axis=0, axis_index_groups=z_groups, tiled=True)

        w_mix = fetch((w_branch, w_recur))
        gates = jnp.stack([w_decay, w_input]).reshape(2, G, heads, -1)
        sends = unxor([gates[:, j] for j in range(G)], g)
        got = [sends[0]] + [flip(sends[d], d) for d in range(1, G)]
        gates = jnp.stack(unxor(got, g))
        gates = gather_far(gates, z).reshape(n, 2, heads, -1)
        gates = jnp.transpose(gates, (1, 2, 0, 3)).reshape(2, heads, BW, BW)
        wg = [
            sum(
                jnp.pad(gates[q, h], ((h * BW, wide - (h + 1) * BW), (h * BW, wide - (h + 1) * BW)))
                for h in range(heads)
            )
            for q in range(2)
        ]
        wg = jnp.concatenate(wg, axis=1)
        w_mix = jnp.concatenate(
            [jnp.pad(w, ((0, 0), (0, wide - ch))) for w in (w_mix[:, :ch], w_mix[:, ch:])], axis=1
        )
        w_out_t = jnp.pad(fetch((w_out.T,)), ((0, 0), (0, wide - ch)))
        w_in = fetch((w_gate, w_up))
        w_down_t = fetch((w_down.T,))
        c_all = gather8(c_own)

        half = G * row
        x_float = x_all.astype(F32)
        normed_mix = rms_scale(x_float, mixer_gain_f).astype(BF)
        mix = dot(normed_mix, w_mix, 1, 0)
        mixed, values, pre, h_all = forward_call(mix, mask, par_f, wg)
        x_own_f = x_own.astype(F32)
        after_mix = x_own_f + scatter8(
            lambda h: dot(mixed[h * half : (h + 1) * half], w_out_t, 1, 1), row
        )
        normed_own = rms_scale(after_mix, mlp_gain_f).astype(BF)
        normed_mlp = gather8(normed_own)
        gate_up = dot(normed_mlp, w_in, 1, 0)
        gate_pre, up_pre = gate_up[:, :ff], gate_up[:, ff:]
        hidden = (jax.nn.gelu(gate_pre) * up_pre).astype(BF)
        result = after_mix + scatter8(
            lambda h: dot(hidden[h * half : (h + 1) * half], w_down_t, 1, 1), row
        )

        grad_down = dot(c_all, hidden, 0, 0)
        grad_hidden = dot(c_all, w_down_t, 1, 0)
        _, pull = jax.vjp(lambda a, b: jax.nn.gelu(a) * b, gate_pre, up_pre)
        grad_gate_pre, grad_up_pre = pull(grad_hidden)
        low = jnp.concatenate([grad_gate_pre.astype(BF), grad_up_pre.astype(BF)], axis=1)
        grad_in = dot(normed_mlp, low, 0, 0)
        grad_normed = scatter8(lambda h: dot(low[h * half : (h + 1) * half], w_in, 1, 1), row)
        _, pull = jax.vjp(rms_scale, after_mix, mlp_gain_f)
        grad_after, grad_mlp_gain = pull(grad_normed)
        grad_after = c_own.astype(F32) + grad_after
        after_low = gather8(grad_after.astype(BF))
        grad_out = dot(after_low, mixed, 0, 0)[:, :ch]
        grad_mixed = dot(after_low, w_out_t, 1, 0)

        mix_low, gate_low, acc = backward_call(mix, grad_mixed, mask, par_f, wg, values, pre, h_all)
        grad_gates = dot(values, gate_low, 0, 0)
        grad_gates = jnp.stack(
            [
                grad_gates[h * BW : (h + 1) * BW, q * wide + h * BW : q * wide + (h + 1) * BW]
                for q in range(2)
                for h in range(heads)
            ]
        )
        acc = jnp.sum(acc, axis=1)[:, :ch]
        chan_grad = jnp.concatenate(
            [acc[: taps + 2], acc[taps + 2 :] * (8.0 * jax.nn.sigmoid(-chan[taps + 2 :]))], axis=0
        )
        grad_mix = dot(normed_mix, mix_low, 0, 0)
        grad_mix = jnp.concatenate([grad_mix[:, :ch], grad_mix[:, wide : wide + ch]], axis=1)
        grad_normed_mix = scatter8(
            lambda h: dot(mix_low[h * half : (h + 1) * half], w_mix, 1, 1), row
        )
        _, pull = jax.vjp(rms_scale, x_own_f, mixer_gain_f)
        grad_x, grad_mix_gain = pull(grad_normed_mix)
        input_grad_own = grad_after + grad_x

        def give(grad, sizes):
            piece = lax.psum_scatter(
                grad.astype(BF), "dp", scatter_dimension=0, axis_index_groups=z_groups, tiled=True
            )
            sends = unxor([piece[j * depth : (j + 1) * depth] for j in range(G)], g)
            got = [sends[0]] + [flip(sends[d], d) for d in range(1, G)]
            got = [a.astype(F32) for a in unxor(got, g)]
            outs, at = [], 0
            for size in sizes:
                outs.append(jnp.concatenate([a[:, at : at + size] for a in got], axis=1))
                at += size
            return outs

        (out_down,) = give(grad_down, (ff,))
        out_gate, out_up = give(grad_in, (ff, ff))
        (out_out,) = give(grad_out, (ch,))
        out_branch, out_recur = give(grad_mix, (ch, ch))
        flat = jnp.transpose(grad_gates.reshape(2, heads, n, -1), (2, 0, 1, 3))
        piece = sum_far(flat.reshape((far, G) + flat.shape[1:]), z, lambda v: v.astype(BF)).astype(BF)
        sends = unxor([piece[j] for j in range(G)], g)
        got = unxor([sends[0]] + [flip(sends[d], d) for d in range(1, G)], g)
        got = jnp.concatenate(got, axis=1).astype(F32)
        out_decay, out_input = got[0], got[1]

        placed = jnp.concatenate([jnp.where(g == j, chan_grad, 0.0) for j in range(G)], axis=1)
        placed = jnp.transpose(placed.reshape(taps + 3, n, part), (1, 0, 2)).reshape(n, -1)
        packed = jnp.concatenate(
            [grad_mix_gain.reshape(n, depth), grad_mlp_gain.reshape(n, depth), placed], axis=1
        )
        packed = sum_far(packed.reshape(far, G, -1), z)
        sends = unxor([packed[j] for j in range(G)], g)
        packed = sends[0]
        for d in range(1, G):
            packed = packed + flip(sends[d], d)
        gains = packed[: 2 * depth]
        gains = gains + swap_core(gains)
        chan_out = packed[2 * depth :].reshape(taps + 3, part)

        def both_rows(own):
            other = swap_core(own)
            first = jnp.where(mp == 0, own, other)
            second = jnp.where(mp == 0, other, own)
            return jnp.stack([first, second])[:, None]

        return (
            both_rows(result),
            both_rows(input_grad_own),
            gains[:depth],
            gains[depth:],
            out_branch,
            out_recur,
            chan_out[:taps],
            out_decay,
            out_input,
            chan_out[taps : taps + 2],
            chan_out[taps + 2],
            out_out.T,
            out_gate,
            out_up,
            out_down.T,
        )

    return body


def solution(mesh):
    in_specs = (
        P(None, "dp", None, None),
        P(None, "dp", None),
        P(None, "dp", None, None),
        P("dp"),
        P("dp"),
        P("dp", "mp"),
        P("dp", "mp"),
        P(None, ("mp", "dp")),
        P("mp", "dp"),
        P("mp", "dp"),
        P(None, ("mp", "dp")),
        P(("mp", "dp")),
        P("mp", "dp"),
        P("dp", "mp"),
        P("dp", "mp"),
        P("mp", "dp"),
    )
    out_specs = (
        P(None, "dp", None, None),
        P(None, "dp", None, None),
        P("dp"),
        P("dp"),
        P("dp", "mp"),
        P("dp", "mp"),
        P(None, ("mp", "dp")),
        P("mp", "dp"),
        P("mp", "dp"),
        P(None, ("mp", "dp")),
        P(("mp", "dp")),
        P("mp", "dp"),
        P("dp", "mp"),
        P("dp", "mp"),
        P("mp", "dp"),
    )
    body = make_body(mesh.shape["dp"], mesh.shape["mp"])
    return jax.shard_map(body, mesh=mesh, in_specs=in_specs, out_specs=out_specs, check_vma=False)
```

```python
import functools

import jax
import jax.numpy as jnp
from jax import lax
from jax.experimental import pallas as pl
from jax.experimental.pallas import tpu as pltpu
from jax.sharding import PartitionSpec as P

BW = 160
G = 4
BF = jnp.bfloat16
F32 = jnp.float32
ROWS = 8
HALF = ROWS // 2
PAD = 8
C0 = 0.7978845608028654
C1 = 0.044715


def sigmoid(v):
    return 0.5 * jnp.tanh(0.5 * v) + 0.5


def gates(dec, inp, sp8, keep):
    r = sigmoid(dec)
    i = sigmoid(inp)
    log_decay = r * sp8
    a = jnp.exp(log_decay)
    gap = -jnp.tanh(log_decay) * (1.0 + a * a)
    return r, i, a, gap


def forward_kernel(cp, row, unroll, extra, near_hbm, far_hbm, mask_ref, par_ref, wg_ref, *refs):
    mixed_ref, values_ref, pre_ref, h_ref, vals, mixf, mix, sems = refs[extra:]
    lanes = cp // 128
    order = list(range(lanes, 2 * lanes)) + list(range(lanes))
    copies = {
        j: [pltpu.make_async_copy((near_hbm, far_hbm)[r // HALF].at[pl.ds(r % HALF * row, row), pl.ds(128 * j, 128)], mix.at[j, pl.ds(r * (row + PAD), row)], sems.at[j, r]) for r in range(ROWS)] for j in order
    }
    for j in order:
        for c in copies[j]:
            c.start()

    def at(ref, t, off=0):
        return [ref[off + j, pl.ds(t, ROWS, stride=row + PAD), :] for j in range(lanes)]

    def put(ref, t, tiles):
        for j in range(lanes):
            ref[j, pl.ds(t, ROWS, stride=row + PAD), :] = tiles[j]

    def flat(ref, rows):
        return jnp.concatenate([ref[j, rows, :] for j in range(lanes)], axis=1)

    def mask(k, t):
        return mask_ref[k, pl.ds(pl.multiple_of(t * ROWS, ROWS), ROWS), :]

    par = [[par_ref[p, :, pl.ds(128 * j, 128)] for j in range(lanes)] for p in range(7)]
    zero = [jnp.zeros((ROWS, 128), F32)] * lanes
    for j in order[:lanes]:
        for c in copies[j]:
            c.wait()

    def conv_step(blk, carry):
        prev = [list(carry[0:lanes]), list(carry[lanes:2 * lanes]), list(carry[2 * lanes:])]
        for u in range(unroll):
            t = blk * unroll + u
            now = at(mix, t, lanes)
            same = [mask(k, t) for k in range(3)]
            out = []
            for j in range(lanes):
                s = now[j] * par[0][j]
                for k in range(3):
                    s = s + par[k + 1][j] * prev[k][j] * same[k]
                out.append(s)
            put(vals, t, out)
            prev = [now, prev[0], prev[1]]
        return tuple(prev[0] + prev[1] + prev[2])

    lax.fori_loop(0, row // unroll, conv_step, tuple(zero * 3))

    for r in range(ROWS):
        rows = pl.ds(r * row, row)
        prow = pl.ds(r * (row + PAD), row)
        low = flat(vals, prow).astype(BF)
        values_ref[rows, :] = low
        pre = jnp.dot(low, wg_ref[...], preferred_element_type=F32)
        for j in range(2 * lanes):
            pre_ref[j, prow, :] = pre[:, 128 * j : 128 * (j + 1)]
    for j in order[lanes:]:
        for c in copies[j]:
            c.wait()

    def step(blk, carry):
        h = list(carry)
        for u in range(unroll):
            t = blk * unroll + u
            dec, inp, val, br = at(pre_ref, t), at(pre_ref, t, lanes), at(vals, t), at(mix, t)
            keep = mask(0, t)
            out = []
            for j in range(lanes):
                r, i, a, gap = gates(dec[j] + par[4][j], inp[j] + par[5][j], par[6][j], keep)
                m = (1.0 - keep) + keep * jnp.sqrt(jnp.maximum(gap, 0.0))
                v = val[j].astype(BF).astype(F32)
                h[j] = a * keep * h[j] + m * i * v
                b = br[j]
                tt = jnp.tanh(C0 * (b + C1 * b * b * b))
                out.append(h[j] * (0.5 * b * (1.0 + tt)))
            put(h_ref, t, h)
            put(mixf, t, out)
        return tuple(h)

    lax.fori_loop(0, row // unroll, step, tuple(zero))
    for r in range(ROWS):
        rows = pl.ds(r * row, row)
        mixed_ref[rows, :] = flat(mixf, pl.ds(r * (row + PAD), row)).astype(BF)


def forward_call(near, far, mask, par, wg, *earlier, unroll=8):
    tokens, cp = 2 * near.shape[0], near.shape[1] // 2
    row = tokens // ROWS
    lanes = cp // 128
    vm = pl.BlockSpec(memory_space=pltpu.VMEM)
    hbm = pl.BlockSpec(memory_space=pl.ANY)
    return pl.pallas_call(
        functools.partial(forward_kernel, cp, row, unroll, len(earlier)),
        in_specs=[hbm] * 2 + [vm] * 3 + [hbm] * len(earlier),
        out_specs=(vm, vm, vm, vm),
        out_shape=(
            jax.ShapeDtypeStruct((tokens, cp), BF),
            jax.ShapeDtypeStruct((tokens, cp), BF),
            jax.ShapeDtypeStruct((2 * lanes, tokens + ROWS * PAD, 128), F32),
            jax.ShapeDtypeStruct((lanes, tokens + ROWS * PAD, 128), F32),
        ),
        scratch_shapes=[
            pltpu.VMEM((lanes, tokens + ROWS * PAD, 128), F32),
            pltpu.VMEM((lanes, tokens + ROWS * PAD, 128), F32),
            pltpu.VMEM((2 * lanes, tokens + ROWS * PAD, 128), F32),
            pltpu.SemaphoreType.DMA((2 * lanes, ROWS)),
        ],
        compiler_params=pltpu.CompilerParams(vmem_limit_bytes=60 * 1024 * 1024),
        cost_estimate=pl.CostEstimate(flops=150 * tokens * cp, bytes_accessed=84 * tokens * cp, transcendentals=6 * tokens * cp),
        name="recur_forward",
    )(near, far, mask, par, wg, *earlier)


def backward_kernel(
    cp, row, unroll, extra, mix_near, mix_far, gm_near, gm_far, mask_ref, par_ref, wg_ref, values_ref, pre_ref, h_ref,
    *refs,
):
    mixlow_ref, low_ref, acc_ref, vals, mix, gm, gdec, ginp, gval, sems = refs[extra:]
    lanes = cp // 128
    pitch = row + PAD
    copies = []
    for j in range(lanes):
        for r in range(ROWS):
            src = pl.ds(r % HALF * row, row)
            mix_hbm, gm_hbm = ((mix_near, gm_near), (mix_far, gm_far))[r // HALF]
            dst = pl.ds(r * pitch, row)
            cols = pl.ds(128 * j, 128)
            rec = pl.ds(cp + 128 * j, 128)
            copies.append(pltpu.make_async_copy(mix_hbm.at[src, cols], mix.at[j, dst], sems.at[0, j, r]))
            copies.append(
                pltpu.make_async_copy(mix_hbm.at[src, rec], mix.at[lanes + j, dst], sems.at[1, j, r])
            )
            copies.append(pltpu.make_async_copy(gm_hbm.at[src, cols], gm.at[j, dst], sems.at[2, j, r]))
    for c in copies:
        c.start()

    def at(ref, t, off=0):
        return [ref[off + j, pl.ds(t, ROWS, stride=pitch), :] for j in range(lanes)]

    def put(ref, t, tiles):
        for j in range(lanes):
            ref[j, pl.ds(t, ROWS, stride=pitch), :] = tiles[j]

    def flat(ref, rows):
        return jnp.concatenate([ref[j, rows, :] for j in range(lanes)], axis=1)

    def mask(k, t):
        return mask_ref[k, pl.ds(pl.multiple_of(t * ROWS, ROWS), ROWS), :]

    par = [[par_ref[p, :, pl.ds(128 * j, 128)] for j in range(lanes)] for p in range(7)]
    zero = [jnp.zeros((ROWS, 128), F32)] * lanes
    for r in range(ROWS):
        low = values_ref[pl.ds(r * row, row), :].astype(F32)
        for j in range(lanes):
            vals[j, pl.ds(r * pitch, row), :] = low[:, 128 * j : 128 * (j + 1)]
    for c in copies:
        c.wait()

    def step(blk, carry):
        carry = [list(carry[lanes * p : lanes * (p + 1)]) for p in range(4)]
        ag, sum_dec, sum_inp, sum_raw = carry
        for u in range(unroll):
            t = row - 1 - (blk * unroll + u)
            dec, inp, val = at(pre_ref, t), at(pre_ref, t, lanes), at(vals, t)
            br, up, here, before = at(mix, t), at(gm, t), at(h_ref, t), at(h_ref, jnp.maximum(t - 1, 0))
            keep = mask(0, t)
            out_b, out_d, out_i, out_v = [], [], [], []
            for j in range(lanes):
                r, i, a, gap = gates(dec[j] + par[4][j], inp[j] + par[5][j], par[6][j], keep)
                gap = jnp.maximum(gap, 1e-30)
                inv = lax.rsqrt(gap)
                m = (1.0 - keep) + keep * (gap * inv)
                b = br[j]
                sq = b * b
                tt = jnp.tanh(C0 * (b + C1 * b * sq))
                half = 0.5 * (1.0 + tt)
                slope = half + 0.5 * b * (1.0 - tt * tt) * (C0 + 3.0 * C0 * C1 * sq)
                g = up[j] * (b * half) + ag[j]
                gi = g * i
                decay = a * keep
                g_log = g * before[j] * decay - gi * val[j] * keep * (a * a * inv)
                ag[j] = decay * g
                gr = g_log * r
                g_dec = gr * par[6][j] * (1.0 - r)
                g_dir = gi * m
                g_inp = g_dir * val[j] * (1.0 - i)
                sum_raw[j] = sum_raw[j] + gr
                sum_dec[j] = sum_dec[j] + g_dec
                sum_inp[j] = sum_inp[j] + g_inp
                out_b.append(up[j] * here[j] * slope)
                out_d.append(g_dec)
                out_i.append(g_inp)
                out_v.append(g_dir)
            put(gm, t, out_b)
            put(gdec, t, out_d)
            put(ginp, t, out_i)
            put(gval, t, out_v)
        return tuple(ag + sum_dec + sum_inp + sum_raw)

    sums = lax.fori_loop(0, row // unroll, step, tuple(zero * 4))
    for p in range(3):
        for j in range(lanes):
            acc_ref[4 + p, :, pl.ds(128 * j, 128)] = sums[lanes * (p + 1) + j]

    for r in range(ROWS):
        rows = pl.ds(r * row, row)
        prow = pl.ds(r * pitch, row)
        low = jnp.concatenate([flat(gdec, prow), flat(ginp, prow)], axis=1).astype(BF)
        low_ref[rows, :] = low
        back = lax.dot_general(low, wg_ref[...], (((1,), (1,)), ((), ())), preferred_element_type=F32)
        for j in range(lanes):
            gval[j, prow, :] = gval[j, prow, :] + back[:, 128 * j : 128 * (j + 1)]
        mixlow_ref[rows, pl.ds(0, cp)] = flat(gm, prow).astype(BF)

    def conv_step(blk, carry):
        carry = [list(carry[lanes * p : lanes * (p + 1)]) for p in range(10)]
        late, sums = carry[:6], carry[6:]
        for u in range(unroll):
            t = row - 1 - (blk * unroll + u)
            now, rec = at(gval, t), at(mix, t, lanes)
            same = [mask(k, t) for k in range(3)]
            taps = [now, late[0], late[1], late[3]]
            out = []
            for j in range(lanes):
                s = par[0][j] * now[j]
                for k in range(1, 4):
                    s = s + par[k][j] * taps[k][j]
                out.append(s)
                for k in range(4):
                    sums[k][j] = sums[k][j] + rec[j] * taps[k][j]
            put(gdec, t, out)
            scaled = [[now[j] * same[k] for j in range(lanes)] for k in range(3)]
            late = [scaled[0], late[2], scaled[1], late[4], late[5], scaled[2]]
        return tuple(sum(late + sums, []))

    sums = lax.fori_loop(0, row // unroll, conv_step, tuple(zero * 10))
    for k in range(4):
        for j in range(lanes):
            acc_ref[k, :, pl.ds(128 * j, 128)] = sums[lanes * (6 + k) + j]
    for r in range(ROWS):
        mixlow_ref[pl.ds(r * row, row), pl.ds(cp, cp)] = flat(gdec, pl.ds(r * pitch, row)).astype(BF)


def backward_call(mix, gm, mask, par, wg, values, pre, h, *earlier, unroll=4):
    tokens, cp = 2 * gm[0].shape[0], gm[0].shape[1]
    row = tokens // ROWS
    lanes = cp // 128
    vm = pl.BlockSpec(memory_space=pltpu.VMEM)
    hbm = pl.BlockSpec(memory_space=pl.ANY)
    slab = pltpu.VMEM((lanes, tokens + ROWS * PAD, 128), F32)
    return pl.pallas_call(
        functools.partial(backward_kernel, cp, row, unroll, len(earlier)),
        in_specs=[hbm] * 4 + [vm] * 6 + [hbm] * len(earlier),
        out_specs=(vm, vm, vm),
        out_shape=(
            jax.ShapeDtypeStruct((tokens, 2 * cp), BF),
            jax.ShapeDtypeStruct((tokens, 2 * cp), BF),
            jax.ShapeDtypeStruct((7, ROWS, cp), F32),
        ),
        scratch_shapes=[
            slab,
            pltpu.VMEM((2 * lanes, tokens + ROWS * PAD, 128), F32),
            slab,
            slab,
            slab,
            slab,
            pltpu.SemaphoreType.DMA((3, lanes, ROWS)),
        ],
        compiler_params=pltpu.CompilerParams(vmem_limit_bytes=60 * 1024 * 1024),
        cost_estimate=pl.CostEstimate(flops=200 * tokens * cp, bytes_accessed=128 * tokens * cp, transcendentals=6 * tokens * cp),
        name="recur_backward",
    )(*mix, *gm, mask, par, wg, values, pre, h, *earlier)


def rms_scale(values, norm_gain):
    return values * lax.rsqrt(jnp.mean(values * values, axis=-1, keepdims=True) + 1e-06) * norm_gain


def same_masks(seg_rows, tap_count):
    same_seg = []
    for offset in range(1, tap_count):
        matched = (seg_rows[..., offset:] == seg_rows[..., :-offset]).astype(F32)
        leading = jnp.zeros(seg_rows.shape[:-1] + (offset,), F32)
        same_seg.append(jnp.concatenate([leading, matched], axis=-1))
    return jnp.stack(same_seg)


def dot(a, b, ca, cb, out=F32):
    return lax.dot_general(a, b, (((ca,), (cb,)), ((), ())), preferred_element_type=out)


def make_body(n, m):
    far = n // G
    planes = [[G * k + c for c in range(G)] for k in range(far)]
    lines = [[c + G * k for k in range(far)] for c in range(G)]
    cores = [(0, 1), (1, 0)]

    def trade(a, groups=planes):
        return lax.all_to_all(a, "dp", 0, 0, axis_index_groups=groups, tiled=True)

    def spread(a, groups=planes):
        return trade(jnp.broadcast_to(a, (len(groups[0]),) + a.shape), groups)

    def swap_core(a):
        return lax.ppermute(a, "mp", cores)

    def pick(a, i):
        return lax.dynamic_index_in_dim(a, i, 0, keepdims=False)

    def index_zero(*earlier):
        total = jnp.int32(0)
        for a in earlier:
            e = a[(0,) * a.ndim]
            total = total + (e != e).astype(jnp.int32)
        return total

    def zero(*earlier):
        return index_zero(*earlier).astype(F32)

    def body(
        inputs,
        segment_ids,
        cotangent,
        mixer_gain,
        mlp_gain,
        w_branch,
        w_recur,
        conv_w,
        w_decay,
        w_input,
        gate_bias,
        decay_param,
        w_out,
        w_gate,
        w_up,
        w_down,
    ):
        dp = lax.axis_index("dp")
        mp = lax.axis_index("mp")
        g = dp % G
        micro, _, row, width = inputs.shape
        depth = width // n
        ch = w_branch.shape[1] // G
        ff = w_gate.shape[1] // G
        heads = w_decay.shape[0] // G
        taps = conv_w.shape[0]
        part = conv_w.shape[1]
        wide = -(-ch // 128) * 128
        half = G * row

        def own_part(a, *earlier):
            return lax.dynamic_index_in_dim(a, mp + index_zero(*earlier), 0, keepdims=False)[0]

        def gather4(own):
            return spread(own).reshape(half, -1)

        def scatter4(sums):
            return jnp.sum(trade(sums.reshape(G, row, -1)).astype(F32), axis=0)

        def halves(a):
            return a[:half], a[half:]

        def token_sum(left, right):
            return dot(left[0], right[0], 0, 0) + dot(left[1], right[1], 0, 0)

        def scatter_z(grad):
            return lax.psum_scatter(grad, "dp", scatter_dimension=0, axis_index_groups=lines, tiled=True)

        def gather_z(rows):
            return lax.all_gather(rows, "dp", axis=0, axis_index_groups=lines, tiled=True)

        def by_column(weights):
            split = [jnp.swapaxes(w.reshape(depth, G, -1), 0, 1) for w in weights]
            return jnp.concatenate(split, axis=2)

        small = [a.reshape(-1) for a in (mixer_gain, mlp_gain, conv_w, gate_bias, decay_param)]
        small = jnp.concatenate(small + [segment_ids.astype(BF).reshape(-1)])
        small_size = small.shape[0] - micro * row
        gate_width = w_decay.shape[1]
        gate_rows = 2 * heads
        small_rows = -(-small.shape[0] // gate_width)
        small = jnp.pad(small, (0, small_rows * gate_width - small.shape[0]))
        pack = [w.reshape(G, heads * gate_width) for w in (w_decay, w_input)]
        pack = jnp.concatenate(pack + [jnp.broadcast_to(small, (G,) + small.shape)], axis=1)
        pack_size = pack.shape[1]
        first = by_column((w_branch, w_recur, w_out.T, w_down.T))
        columns = first.shape[2]
        pack_rows = -(-pack_size // columns)
        pack = jnp.pad(pack, ((0, 0), (0, pack_rows * columns - pack_size)))
        first = trade(jnp.concatenate([first, pack.reshape(G, pack_rows, columns)], axis=1))
        mix_rows = first[:, :depth, : 3 * ch].reshape(G * depth, -1)
        w_down_rows = first[:, :depth, 3 * ch :].reshape(G * depth, -1)
        pack = first[:, depth:].reshape(G, -1)[:, :pack_size].reshape(G, gate_rows + small_rows, gate_width)
        seg_rows = pack[:, gate_rows:].reshape(G, -1)[:, small_size : small_size + micro * row]
        seg_rows = jnp.swapaxes(seg_rows.reshape(G, micro, row), 0, 1)
        seg_all = jnp.concatenate([pick(seg_rows, mp), pick(seg_rows, 1 - mp)], axis=0)
        packs = spread(pack, lines).reshape(n, gate_rows + small_rows, gate_width)
        small = packs[:, gate_rows:].reshape(n, -1)[:, :small_size].astype(F32)
        mixer_gain_f = small[:, :depth].reshape(width)
        mlp_gain_f = small[:, depth : 2 * depth].reshape(width)
        chan = small[:, 2 * depth :].reshape(n, taps + 3, part)
        chan = jnp.transpose(chan, (1, 0, 2)).reshape(taps + 3, n * part)
        chan = lax.dynamic_slice_in_dim(chan, g * ch, ch, 1)
        gates = packs[:, :gate_rows].reshape(n, 2, heads, -1)
        gates = jnp.transpose(gates, (1, 2, 0, 3)).reshape(2, heads, BW, BW)
        wg = [
            sum(
                jnp.pad(gates[q, h], ((h * BW, wide - (h + 1) * BW), (h * BW, wide - (h + 1) * BW)))
                for h in range(heads)
            )
            for q in range(2)
        ]
        wg = jnp.concatenate(wg, axis=1)
        sp8 = -8.0 * jax.nn.softplus(-chan[taps + 2 :])
        par = jnp.concatenate(
            [
                jnp.pad(chan[: taps + 2], ((0, 0), (0, wide - ch))),
                jnp.pad(sp8, ((0, 0), (0, wide - ch)), constant_values=-1.0),
            ],
            axis=0,
        )
        par_f = jnp.broadcast_to(par[:, None], (taps + 3, ROWS, wide))
        mask = jnp.transpose(same_masks(seg_all, taps), (0, 2, 1)).reshape(taps - 1, ROWS * row, 1)
        mask = jnp.broadcast_to(mask, (taps - 1, ROWS * row, 128))

        rows = gather_z(mix_rows)
        w_down_t = gather_z(w_down_rows)
        x_own_f = own_part(inputs).astype(F32)
        normed_own = rms_scale(x_own_f, mixer_gain_f)
        normed_near = gather4(normed_own.astype(BF))
        normed_mix = [normed_near, swap_core(normed_near)]
        c_near = gather4(own_part(cotangent, normed_near))
        c_half = [c_near, swap_core(c_near)]
        w_in_rows = trade(by_column((w_gate, w_up))).reshape(G * depth, -1)
        w_in = gather_z(w_in_rows)
        w_mix = jnp.concatenate(
            [jnp.pad(w, ((0, 0), (0, wide - ch))) for w in (rows[:, :ch], rows[:, ch : 2 * ch])], axis=1
        ) + zero(w_in_rows).astype(BF)
        w_out_t = jnp.pad(rows[:, 2 * ch :], ((0, 0), (0, wide - ch)))

        mix = [dot(a, w_mix, 1, 0) for a in normed_mix]
        mixed, values, pre, h_all = forward_call(*mix, mask, par_f, wg)
        mixed_near, mixed_far = halves(mixed)
        c_part = c_near[:, :wide]
        mixed_far = mixed_far + (c_part != c_part).astype(BF)
        arrived = swap_core(dot(mixed_far, w_out_t, 1, 1, BF))
        sums = dot(mixed_near, w_out_t, 1, 1) + arrived.astype(F32)
        after_mix = x_own_f + scatter4(sums.astype(BF))
        normed_own = (rms_scale(after_mix, mlp_gain_f) + zero(w_in)).astype(BF)
        normed_near = gather4(normed_own)
        normed = [normed_near, swap_core(normed_near + zero(w_down_t).astype(BF))]
        hidden, gate_up = [], []
        for a in normed:
            pre_act = dot(a, w_in, 1, 0)
            gate_up.append(pre_act)
            hidden.append((jax.nn.gelu(pre_act[:, :ff]) * pre_act[:, ff:]).astype(BF))

        grad_down = token_sum(c_half, hidden).astype(BF)
        down_piece = scatter_z(grad_down)
        low = []
        for c_part, pre_act in zip(c_half, gate_up):
            grad_hidden = dot(c_part, w_down_t, 1, 0)
            _, pull = jax.vjp(lambda a, b: jax.nn.gelu(a) * b, pre_act[:, :ff], pre_act[:, ff:])
            low.append(jnp.concatenate([(a + zero(grad_down)).astype(BF) for a in pull(grad_hidden)], axis=1))
        arrived = swap_core(dot(low[1], w_in, 1, 1, BF))
        sums = (dot(low[0], w_in, 1, 1) + arrived.astype(F32)).astype(BF)
        low_all = jnp.concatenate([a + zero(sums).astype(BF) for a in low], axis=0)
        grad_in = dot(jnp.concatenate(normed, axis=0), low_all, 0, 0).astype(BF)
        in_piece = scatter_z(grad_in)
        hidden = [a + zero(sums).astype(BF) for a in hidden]
        arrived = swap_core(dot(hidden[1], w_down_t, 1, 1, BF))
        result_sums = (dot(hidden[0], w_down_t, 1, 1) + arrived.astype(F32)).astype(BF)
        grad_normed = scatter4(sums) + zero(grad_in, down_piece, result_sums)
        _, pull = jax.vjp(rms_scale, after_mix, mlp_gain_f)
        grad_after, grad_mlp_gain = pull(grad_normed)
        grad_after = own_part(cotangent).astype(F32) + grad_after
        after_own = grad_after.astype(BF)
        after_near = gather4(after_own)
        after_low = [after_near, swap_core(after_near)]
        grad_mixed = [dot(a, w_out_t, 1, 0) for a in after_low]
        grad_out = token_sum(after_low, (mixed_near, mixed_far))
        grad_out = grad_out[:, :ch].astype(BF)

        out_piece = scatter_z(grad_out)
        mix_low, gate_low, acc = backward_call(
            mix, grad_mixed, mask, par_f, wg, values, pre, h_all, grad_out, result_sums
        )
        result = after_mix + scatter4(result_sums) + zero(mix_low)
        low_near, low_far = halves(mix_low)
        arrived = swap_core(dot(low_far, w_mix, 1, 1, BF))
        sums = (dot(low_near, w_mix, 1, 1) + arrived.astype(F32) + zero(result)).astype(BF)
        behind = zero(sums).astype(BF)
        grad_mix = token_sum(normed_mix, halves(mix_low + behind))
        gate_low = gate_low + behind
        grad_mix = jnp.concatenate([grad_mix[:, :ch], grad_mix[:, wide : wide + ch]], axis=1).astype(BF)

        grad_gates = dot(values, gate_low, 0, 0)
        grad_gates = jnp.stack(
            [
                grad_gates[h * BW : (h + 1) * BW, q * wide + h * BW : q * wide + (h + 1) * BW]
                for q in range(2)
                for h in range(heads)
            ]
        )
        grad_gates = jnp.swapaxes(grad_gates.reshape(gate_rows, n, gate_width), 0, 1).reshape(n, -1)
        acc = jnp.sum(acc, axis=1)[:, :ch]
        chan_grad = jnp.concatenate(
            [acc[: taps + 2], acc[taps + 2 :] * (8.0 * jax.nn.sigmoid(-chan[taps + 2 :]))], axis=0
        )
        chan_grad = jnp.concatenate([jnp.where(g == j, chan_grad, 0.0) for j in range(G)], axis=1)
        chan_grad = jnp.transpose(chan_grad.reshape(taps + 3, n, part), (1, 0, 2)).reshape(n, -1)
        extra = jnp.concatenate([grad_gates, chan_grad, grad_mlp_gain.reshape(n, depth)], axis=1)
        more = -(-extra.shape[1] // (2 * ch))
        extra = jnp.pad(extra, ((0, 0), (0, more * 2 * ch - extra.shape[1]))).astype(BF)
        grad_mix = jnp.concatenate(
            [grad_mix.reshape(n, depth, -1), extra.reshape(n, more, 2 * ch)], axis=1
        )
        mix_piece = scatter_z(grad_mix)
        sums = trade(sums.reshape(G, row, -1))
        grad_normed_mix = jnp.sum(sums.astype(F32), axis=0) + zero(grad_mix, in_piece, out_piece)
        _, pull = jax.vjp(rms_scale, x_own_f, mixer_gain_f)
        grad_x, grad_mix_gain = pull(grad_normed_mix)
        input_grad_own = grad_after + grad_x

        pieces = [p.reshape(G, depth, -1) for p in (down_piece, in_piece, out_piece)]
        got = trade(jnp.concatenate(pieces, axis=2) + zero(sums).astype(BF))
        outs = []
        for at, size in ((0, ff), (ff, ff), (2 * ff, ff), (3 * ff, ch)):
            outs.append(jnp.swapaxes(got[:, :, at : at + size], 0, 1).reshape(depth, -1).astype(F32))
        out_down, out_gate, out_up, out_out = outs
        got = trade(mix_piece)
        out_branch, out_recur = [
            jnp.swapaxes(got[:, :depth, at : at + ch], 0, 1).reshape(depth, -1).astype(F32) for at in (0, ch)
        ]
        got = got[:, depth:].reshape(G, -1)
        gate_size = gate_rows * gate_width
        flat = jnp.swapaxes(got[:, :gate_size].reshape(G, 2, heads, -1), 0, 1)
        flat = flat.reshape(2, G * heads, -1).astype(F32)
        got = jnp.sum(got[:, gate_size : gate_size + (taps + 3) * part + depth].astype(F32), axis=0)
        chan_out = got[: (taps + 3) * part].reshape(taps + 3, part)
        mlp_gain_out = got[(taps + 3) * part :]
        mlp_gain_out = mlp_gain_out + swap_core(mlp_gain_out)
        def sum_flips(a, at, count, step):
            total = pick(a, at)
            for k in range(1, count):
                pairs = [(i, i ^ (k * step)) for i in range(n)]
                total = total + lax.ppermute(pick(a, at ^ k), "dp", pairs)
            return total

        mix_gain_out = sum_flips(grad_mix_gain.reshape(far, G, depth), dp // G, far, G)
        mix_gain_out = sum_flips(mix_gain_out, g, G, 1)
        mix_gain_out = mix_gain_out + swap_core(mix_gain_out)

        def both_rows(own):
            other = swap_core(own)
            first = jnp.where(mp == 0, own, other)
            second = jnp.where(mp == 0, other, own)
            return jnp.stack([first, second])[:, None]

        return (
            both_rows(result),
            both_rows(input_grad_own),
            mix_gain_out,
            mlp_gain_out,
            out_branch,
            out_recur,
            chan_out[:taps],
            flat[0],
            flat[1],
            chan_out[taps : taps + 2],
            chan_out[taps + 2],
            out_out.T,
            out_gate,
            out_up,
            out_down.T,
        )

    return body


def solution(mesh):
    in_specs = (
        P(None, "dp", None, None),
        P(None, "dp", None),
        P(None, "dp", None, None),
        P("dp"),
        P("dp"),
        P("dp", "mp"),
        P("dp", "mp"),
        P(None, ("mp", "dp")),
        P("mp", "dp"),
        P("mp", "dp"),
        P(None, ("mp", "dp")),
        P(("mp", "dp")),
        P("mp", "dp"),
        P("dp", "mp"),
        P("dp", "mp"),
        P("mp", "dp"),
    )
    out_specs = (
        P(None, "dp", None, None),
        P(None, "dp", None, None),
        P("dp"),
        P("dp"),
        P("dp", "mp"),
        P("dp", "mp"),
        P(None, ("mp", "dp")),
        P("mp", "dp"),
        P("mp", "dp"),
        P(None, ("mp", "dp")),
        P(("mp", "dp")),
        P("mp", "dp"),
        P("dp", "mp"),
        P("dp", "mp"),
        P("mp", "dp"),
    )
    body = make_body(mesh.shape["dp"], mesh.shape["mp"])
    return jax.shard_map(body, mesh=mesh, in_specs=in_specs, out_specs=out_specs, check_vma=False)
```

```python
import functools

import jax
import jax.numpy as jnp
from jax import lax
from jax.experimental import pallas as pl
from jax.experimental.pallas import tpu as pltpu
from jax.sharding import PartitionSpec as P

BW = 160
G = 4
BF = jnp.bfloat16
F32 = jnp.float32
ROWS = 8
HALF = ROWS // 2
PAD = 8
C0 = 0.7978845608028654
C1 = 0.044715


def sigmoid(v):
    return 0.5 * jnp.tanh(0.5 * v) + 0.5


def gates(dec, inp, sp8, keep):
    r = sigmoid(dec)
    i = sigmoid(inp)
    log_decay = r * sp8
    a = jnp.exp(log_decay)
    gap = -jnp.tanh(log_decay) * (1.0 + a * a)
    return r, i, a, gap


def forward_kernel(cp, row, unroll, extra, near_hbm, far_hbm, mask_ref, par_ref, wg_ref, *refs):
    mixed_ref, values_ref, pre_ref, h_ref, vals, mixf, mix, sems = refs[extra:]
    lanes = cp // 128
    order = list(range(lanes, 2 * lanes)) + list(range(lanes))
    copies = {
        j: [pltpu.make_async_copy((near_hbm, far_hbm)[r // HALF].at[pl.ds(r % HALF * row, row), pl.ds(128 * j, 128)], mix.at[j, pl.ds(r * (row + PAD), row)], sems.at[j, r]) for r in range(ROWS)] for j in order
    }
    for j in order:
        for c in copies[j]:
            c.start()

    def at(ref, t, off=0):
        return [ref[off + j, pl.ds(t, ROWS, stride=row + PAD), :] for j in range(lanes)]

    def put(ref, t, tiles):
        for j in range(lanes):
            ref[j, pl.ds(t, ROWS, stride=row + PAD), :] = tiles[j]

    def flat(ref, rows):
        return jnp.concatenate([ref[j, rows, :] for j in range(lanes)], axis=1)

    def mask(k, t):
        return mask_ref[k, pl.ds(pl.multiple_of(t * ROWS, ROWS), ROWS), :]

    par = [[par_ref[p, :, pl.ds(128 * j, 128)] for j in range(lanes)] for p in range(7)]
    zero = [jnp.zeros((ROWS, 128), F32)] * lanes
    for j in order[:lanes]:
        for c in copies[j]:
            c.wait()

    def conv_step(blk, carry):
        prev = [list(carry[0:lanes]), list(carry[lanes:2 * lanes]), list(carry[2 * lanes:])]
        for u in range(unroll):
            t = blk * unroll + u
            now = at(mix, t, lanes)
            same = [mask(k, t) for k in range(3)]
            out = []
            for j in range(lanes):
                s = now[j] * par[0][j]
                for k in range(3):
                    s = s + par[k + 1][j] * prev[k][j] * same[k]
                out.append(s)
            put(vals, t, out)
            prev = [now, prev[0], prev[1]]
        return tuple(prev[0] + prev[1] + prev[2])

    lax.fori_loop(0, row // unroll, conv_step, tuple(zero * 3))

    for r in range(ROWS):
        rows = pl.ds(r * row, row)
        prow = pl.ds(r * (row + PAD), row)
        low = flat(vals, prow).astype(BF)
        values_ref[rows, :] = low
        pre = jnp.dot(low, wg_ref[...], preferred_element_type=F32)
        for j in range(2 * lanes):
            pre_ref[j, prow, :] = pre[:, 128 * j : 128 * (j + 1)]
    for j in order[lanes:]:
        for c in copies[j]:
            c.wait()

    def step(blk, carry):
        h = list(carry)
        for u in range(unroll):
            t = blk * unroll + u
            dec, inp, val, br = at(pre_ref, t), at(pre_ref, t, lanes), at(vals, t), at(mix, t)
            keep = mask(0, t)
            out = []
            for j in range(lanes):
                r, i, a, gap = gates(dec[j] + par[4][j], inp[j] + par[5][j], par[6][j], keep)
                m = (1.0 - keep) + keep * jnp.sqrt(jnp.maximum(gap, 0.0))
                v = val[j].astype(BF).astype(F32)
                h[j] = a * keep * h[j] + m * i * v
                b = br[j]
                tt = jnp.tanh(C0 * (b + C1 * b * b * b))
                out.append(h[j] * (0.5 * b * (1.0 + tt)))
            put(h_ref, t, h)
            put(mixf, t, out)
        return tuple(h)

    lax.fori_loop(0, row // unroll, step, tuple(zero))
    for r in range(ROWS):
        rows = pl.ds(r * row, row)
        mixed_ref[rows, :] = flat(mixf, pl.ds(r * (row + PAD), row)).astype(BF)


def forward_call(near, far, mask, par, wg, *earlier, unroll=8):
    tokens, cp = 2 * near.shape[0], near.shape[1] // 2
    row = tokens // ROWS
    lanes = cp // 128
    vm = pl.BlockSpec(memory_space=pltpu.VMEM)
    hbm = pl.BlockSpec(memory_space=pl.ANY)
    return pl.pallas_call(
        functools.partial(forward_kernel, cp, row, unroll, len(earlier)),
        in_specs=[hbm] * 2 + [vm] * 3 + [hbm] * len(earlier),
        out_specs=(vm, vm, vm, vm),
        out_shape=(
            jax.ShapeDtypeStruct((tokens, cp), BF),
            jax.ShapeDtypeStruct((tokens, cp), BF),
            jax.ShapeDtypeStruct((2 * lanes, tokens + ROWS * PAD, 128), F32),
            jax.ShapeDtypeStruct((lanes, tokens + ROWS * PAD, 128), F32),
        ),
        scratch_shapes=[
            pltpu.VMEM((lanes, tokens + ROWS * PAD, 128), F32),
            pltpu.VMEM((lanes, tokens + ROWS * PAD, 128), F32),
            pltpu.VMEM((2 * lanes, tokens + ROWS * PAD, 128), F32),
            pltpu.SemaphoreType.DMA((2 * lanes, ROWS)),
        ],
        compiler_params=pltpu.CompilerParams(vmem_limit_bytes=36 * 1024 * 1024),
        cost_estimate=pl.CostEstimate(flops=150 * tokens * cp, bytes_accessed=84 * tokens * cp, transcendentals=6 * tokens * cp),
        name="recur_forward",
    )(near, far, mask, par, wg, *earlier)


def backward_kernel(
    cp, row, unroll, extra, mix_near, mix_far, gm_near, gm_far, mask_ref, par_ref, wg_ref, values_ref, pre_ref, h_ref,
    *refs,
):
    mixlow_ref, low_ref, acc_ref, vals, mix, gm, gdec, ginp, gval, sems = refs[extra:]
    lanes = cp // 128
    pitch = row + PAD
    copies = []
    for j in range(lanes):
        for r in range(ROWS):
            src = pl.ds(r % HALF * row, row)
            mix_hbm, gm_hbm = ((mix_near, gm_near), (mix_far, gm_far))[r // HALF]
            dst = pl.ds(r * pitch, row)
            cols = pl.ds(128 * j, 128)
            rec = pl.ds(cp + 128 * j, 128)
            copies.append(pltpu.make_async_copy(mix_hbm.at[src, cols], mix.at[j, dst], sems.at[0, j, r]))
            copies.append(
                pltpu.make_async_copy(mix_hbm.at[src, rec], mix.at[lanes + j, dst], sems.at[1, j, r])
            )
            copies.append(pltpu.make_async_copy(gm_hbm.at[src, cols], gm.at[j, dst], sems.at[2, j, r]))
    for c in copies:
        c.start()

    def at(ref, t, off=0):
        return [ref[off + j, pl.ds(t, ROWS, stride=pitch), :] for j in range(lanes)]

    def put(ref, t, tiles):
        for j in range(lanes):
            ref[j, pl.ds(t, ROWS, stride=pitch), :] = tiles[j]

    def flat(ref, rows):
        return jnp.concatenate([ref[j, rows, :] for j in range(lanes)], axis=1)

    def mask(k, t):
        return mask_ref[k, pl.ds(pl.multiple_of(t * ROWS, ROWS), ROWS), :]

    par = [[par_ref[p, :, pl.ds(128 * j, 128)] for j in range(lanes)] for p in range(7)]
    zero = [jnp.zeros((ROWS, 128), F32)] * lanes
    for r in range(ROWS):
        low = values_ref[pl.ds(r * row, row), :].astype(F32)
        for j in range(lanes):
            vals[j, pl.ds(r * pitch, row), :] = low[:, 128 * j : 128 * (j + 1)]
    for c in copies:
        c.wait()

    def step(blk, carry):
        carry = [list(carry[lanes * p : lanes * (p + 1)]) for p in range(4)]
        ag, sum_dec, sum_inp, sum_raw = carry
        for u in range(unroll):
            t = row - 1 - (blk * unroll + u)
            dec, inp, val = at(pre_ref, t), at(pre_ref, t, lanes), at(vals, t)
            br, up, here, before = at(mix, t), at(gm, t), at(h_ref, t), at(h_ref, jnp.maximum(t - 1, 0))
            keep = mask(0, t)
            out_b, out_d, out_i, out_v = [], [], [], []
            for j in range(lanes):
                r, i, a, gap = gates(dec[j] + par[4][j], inp[j] + par[5][j], par[6][j], keep)
                gap = jnp.maximum(gap, 1e-30)
                inv = lax.rsqrt(gap)
                m = (1.0 - keep) + keep * (gap * inv)
                b = br[j]
                sq = b * b
                tt = jnp.tanh(C0 * (b + C1 * b * sq))
                half = 0.5 * (1.0 + tt)
                slope = half + 0.5 * b * (1.0 - tt * tt) * (C0 + 3.0 * C0 * C1 * sq)
                g = up[j] * (b * half) + ag[j]
                gi = g * i
                decay = a * keep
                g_log = g * before[j] * decay - gi * val[j] * keep * (a * a * inv)
                ag[j] = decay * g
                gr = g_log * r
                g_dec = gr * par[6][j] * (1.0 - r)
                g_dir = gi * m
                g_inp = g_dir * val[j] * (1.0 - i)
                sum_raw[j] = sum_raw[j] + gr
                sum_dec[j] = sum_dec[j] + g_dec
                sum_inp[j] = sum_inp[j] + g_inp
                out_b.append(up[j] * here[j] * slope)
                out_d.append(g_dec)
                out_i.append(g_inp)
                out_v.append(g_dir)
            put(gm, t, out_b)
            put(gdec, t, out_d)
            put(ginp, t, out_i)
            put(gval, t, out_v)
        return tuple(ag + sum_dec + sum_inp + sum_raw)

    sums = lax.fori_loop(0, row // unroll, step, tuple(zero * 4))
    for p in range(3):
        for j in range(lanes):
            acc_ref[4 + p, :, pl.ds(128 * j, 128)] = sums[lanes * (p + 1) + j]

    for r in range(ROWS):
        rows = pl.ds(r * row, row)
        prow = pl.ds(r * pitch, row)
        low = jnp.concatenate([flat(gdec, prow), flat(ginp, prow)], axis=1).astype(BF)
        low_ref[rows, :] = low
        back = lax.dot_general(low, wg_ref[...], (((1,), (1,)), ((), ())), preferred_element_type=F32)
        for j in range(lanes):
            gval[j, prow, :] = gval[j, prow, :] + back[:, 128 * j : 128 * (j + 1)]
        mixlow_ref[rows, pl.ds(0, cp)] = flat(gm, prow).astype(BF)

    def conv_step(blk, carry):
        carry = [list(carry[lanes * p : lanes * (p + 1)]) for p in range(10)]
        late, sums = carry[:6], carry[6:]
        for u in range(unroll):
            t = row - 1 - (blk * unroll + u)
            now, rec = at(gval, t), at(mix, t, lanes)
            same = [mask(k, t) for k in range(3)]
            taps = [now, late[0], late[1], late[3]]
            out = []
            for j in range(lanes):
                s = par[0][j] * now[j]
                for k in range(1, 4):
                    s = s + par[k][j] * taps[k][j]
                out.append(s)
                for k in range(4):
                    sums[k][j] = sums[k][j] + rec[j] * taps[k][j]
            put(gdec, t, out)
            scaled = [[now[j] * same[k] for j in range(lanes)] for k in range(3)]
            late = [scaled[0], late[2], scaled[1], late[4], late[5], scaled[2]]
        return tuple(sum(late + sums, []))

    sums = lax.fori_loop(0, row // unroll, conv_step, tuple(zero * 10))
    for k in range(4):
        for j in range(lanes):
            acc_ref[k, :, pl.ds(128 * j, 128)] = sums[lanes * (6 + k) + j]
    for r in range(ROWS):
        mixlow_ref[pl.ds(r * row, row), pl.ds(cp, cp)] = flat(gdec, pl.ds(r * pitch, row)).astype(BF)


def backward_call(mix, gm, mask, par, wg, values, pre, h, *earlier, unroll=4):
    tokens, cp = 2 * gm[0].shape[0], gm[0].shape[1]
    row = tokens // ROWS
    lanes = cp // 128
    vm = pl.BlockSpec(memory_space=pltpu.VMEM)
    hbm = pl.BlockSpec(memory_space=pl.ANY)
    slab = pltpu.VMEM((lanes, tokens + ROWS * PAD, 128), F32)
    return pl.pallas_call(
        functools.partial(backward_kernel, cp, row, unroll, len(earlier)),
        in_specs=[hbm] * 4 + [vm] * 6 + [hbm] * len(earlier),
        out_specs=(vm, vm, vm),
        out_shape=(
            jax.ShapeDtypeStruct((tokens, 2 * cp), BF),
            jax.ShapeDtypeStruct((tokens, 2 * cp), BF),
            jax.ShapeDtypeStruct((7, ROWS, cp), F32),
        ),
        scratch_shapes=[
            slab,
            pltpu.VMEM((2 * lanes, tokens + ROWS * PAD, 128), F32),
            slab,
            slab,
            slab,
            slab,
            pltpu.SemaphoreType.DMA((3, lanes, ROWS)),
        ],
        compiler_params=pltpu.CompilerParams(vmem_limit_bytes=48 * 1024 * 1024),
        cost_estimate=pl.CostEstimate(flops=200 * tokens * cp, bytes_accessed=128 * tokens * cp, transcendentals=6 * tokens * cp),
        name="recur_backward",
    )(*mix, *gm, mask, par, wg, values, pre, h, *earlier)


def rms_scale(values, norm_gain):
    return values * lax.rsqrt(jnp.mean(values * values, axis=-1, keepdims=True) + 1e-06) * norm_gain


def same_masks(seg_rows, tap_count):
    same_seg = []
    for offset in range(1, tap_count):
        matched = (seg_rows[..., offset:] == seg_rows[..., :-offset]).astype(F32)
        leading = jnp.zeros(seg_rows.shape[:-1] + (offset,), F32)
        same_seg.append(jnp.concatenate([leading, matched], axis=-1))
    return jnp.stack(same_seg)


def dot(a, b, ca, cb, out=F32):
    return lax.dot_general(a, b, (((ca,), (cb,)), ((), ())), preferred_element_type=out)


def make_body(n, m):
    far = n // G
    planes = [[G * k + c for c in range(G)] for k in range(far)]
    lines = [[c + G * k for k in range(far)] for c in range(G)]
    cores = [(0, 1), (1, 0)]

    def trade(a, groups=planes):
        return lax.all_to_all(a, "dp", 0, 0, axis_index_groups=groups, tiled=True)

    def spread(a, groups=planes):
        return trade(jnp.broadcast_to(a, (len(groups[0]),) + a.shape), groups)

    def swap_core(a):
        return lax.ppermute(a, "mp", cores)

    def pick(a, i):
        return lax.dynamic_index_in_dim(a, i, 0, keepdims=False)

    def index_zero(*earlier):
        total = jnp.int32(0)
        for a in earlier:
            e = a[(0,) * a.ndim]
            total = total + (e != e).astype(jnp.int32)
        return total

    def zero(*earlier):
        return index_zero(*earlier).astype(F32)

    def body(
        inputs,
        segment_ids,
        cotangent,
        mixer_gain,
        mlp_gain,
        w_branch,
        w_recur,
        conv_w,
        w_decay,
        w_input,
        gate_bias,
        decay_param,
        w_out,
        w_gate,
        w_up,
        w_down,
    ):
        dp = lax.axis_index("dp")
        mp = lax.axis_index("mp")
        g = dp % G
        micro, _, row, width = inputs.shape
        depth = width // n
        ch = w_branch.shape[1] // G
        ff = w_gate.shape[1] // G
        heads = w_decay.shape[0] // G
        taps = conv_w.shape[0]
        part = conv_w.shape[1]
        wide = -(-ch // 128) * 128
        half = G * row

        def own_part(a, *earlier):
            return lax.dynamic_index_in_dim(a, mp + index_zero(*earlier), 0, keepdims=False)[0]

        def gather4(own):
            return spread(own).reshape(half, -1)

        def scatter4(sums):
            return jnp.sum(trade(sums.reshape(G, row, -1)).astype(F32), axis=0)

        def halves(a):
            return a[:half], a[half:]

        def token_sum(left, right):
            return dot(left[0], right[0], 0, 0) + dot(left[1], right[1], 0, 0)

        def scatter_z(grad):
            return lax.psum_scatter(grad, "dp", scatter_dimension=0, axis_index_groups=lines, tiled=True)

        def gather_z(rows):
            return lax.all_gather(rows, "dp", axis=0, axis_index_groups=lines, tiled=True)

        def by_column(weights):
            split = [jnp.swapaxes(w.reshape(depth, G, -1), 0, 1) for w in weights]
            return jnp.concatenate(split, axis=2)

        small = [a.reshape(-1) for a in (mixer_gain, mlp_gain, conv_w, gate_bias, decay_param)]
        small = jnp.concatenate(small + [segment_ids.astype(BF).reshape(-1)])
        small_size = small.shape[0] - micro * row
        gate_width = w_decay.shape[1]
        gate_rows = 2 * heads
        small_rows = -(-small.shape[0] // gate_width)
        small = jnp.pad(small, (0, small_rows * gate_width - small.shape[0]))
        pack = [w.reshape(G, heads * gate_width) for w in (w_decay, w_input)]
        pack = jnp.concatenate(pack + [jnp.broadcast_to(small, (G,) + small.shape)], axis=1)
        pack_size = pack.shape[1]
        first = by_column((w_branch, w_recur, w_out.T))
        columns = first.shape[2]
        pack_rows = -(-pack_size // columns)
        pack = jnp.pad(pack, ((0, 0), (0, pack_rows * columns - pack_size)))
        first = trade(jnp.concatenate([first, pack.reshape(G, pack_rows, columns)], axis=1))
        mix_rows = first[:, :depth].reshape(G * depth, -1)
        pack = first[:, depth:].reshape(G, -1)[:, :pack_size].reshape(G, gate_rows + small_rows, gate_width)
        seg_rows = pack[:, gate_rows:].reshape(G, -1)[:, small_size : small_size + micro * row]
        seg_rows = jnp.swapaxes(seg_rows.reshape(G, micro, row), 0, 1)
        seg_all = jnp.concatenate([pick(seg_rows, mp), pick(seg_rows, 1 - mp)], axis=0)
        packs = spread(pack, lines).reshape(n, gate_rows + small_rows, gate_width)
        small = packs[:, gate_rows:].reshape(n, -1)[:, :small_size].astype(F32)
        mixer_gain_f = small[:, :depth].reshape(width)
        mlp_gain_f = small[:, depth : 2 * depth].reshape(width)
        chan = small[:, 2 * depth :].reshape(n, taps + 3, part)
        chan = jnp.transpose(chan, (1, 0, 2)).reshape(taps + 3, n * part)
        chan = lax.dynamic_slice_in_dim(chan, g * ch, ch, 1)
        gates = packs[:, :gate_rows].reshape(n, 2, heads, -1)
        gates = jnp.transpose(gates, (1, 2, 0, 3)).reshape(2, heads, BW, BW)
        wg = [
            sum(
                jnp.pad(gates[q, h], ((h * BW, wide - (h + 1) * BW), (h * BW, wide - (h + 1) * BW)))
                for h in range(heads)
            )
            for q in range(2)
        ]
        wg = jnp.concatenate(wg, axis=1)
        sp8 = -8.0 * jax.nn.softplus(-chan[taps + 2 :])
        par = jnp.concatenate(
            [
                jnp.pad(chan[: taps + 2], ((0, 0), (0, wide - ch))),
                jnp.pad(sp8, ((0, 0), (0, wide - ch)), constant_values=-1.0),
            ],
            axis=0,
        )
        par_f = jnp.broadcast_to(par[:, None], (taps + 3, ROWS, wide))
        mask = jnp.transpose(same_masks(seg_all, taps), (0, 2, 1)).reshape(taps - 1, ROWS * row, 1)
        mask = jnp.broadcast_to(mask, (taps - 1, ROWS * row, 128))

        rows = gather_z(mix_rows)
        x_own_f = own_part(inputs).astype(F32)
        normed_own = rms_scale(x_own_f, mixer_gain_f)
        normed_near = gather4(normed_own.astype(BF))
        normed_mix = [normed_near, swap_core(normed_near)]
        w_in_rows = trade(by_column((w_gate, w_up))).reshape(G * depth, -1)
        w_down_rows = trade(by_column((w_down.T,))).reshape(G * depth, -1)
        w_down_t = gather_z(w_down_rows)
        c_near = gather4(own_part(cotangent, normed_near, w_down_rows))
        c_half = [c_near, swap_core(c_near)]
        w_in = gather_z(w_in_rows)
        w_mix = jnp.concatenate(
            [jnp.pad(w, ((0, 0), (0, wide - ch))) for w in (rows[:, :ch], rows[:, ch : 2 * ch])], axis=1
        ) + zero(w_in_rows).astype(BF)
        w_out_t = jnp.pad(rows[:, 2 * ch :], ((0, 0), (0, wide - ch)))

        mix = [dot(a, w_mix, 1, 0) for a in normed_mix]
        mixed, values, pre, h_all = forward_call(*mix, mask, par_f, wg)
        mixed_near, mixed_far = halves(mixed)
        c_part = c_near[:, :wide]
        mixed_far = mixed_far + (c_part != c_part).astype(BF)
        arrived = swap_core(dot(mixed_far, w_out_t, 1, 1, BF))
        sums = dot(mixed_near, w_out_t, 1, 1) + arrived.astype(F32)
        after_mix = x_own_f + scatter4(sums.astype(BF))
        normed_own = (rms_scale(after_mix, mlp_gain_f) + zero(w_in)).astype(BF)
        normed_near = gather4(normed_own)
        normed = [normed_near, swap_core(normed_near + zero(w_down_t).astype(BF))]
        hidden, gate_up = [], []
        for a in normed:
            pre_act = dot(a, w_in, 1, 0)
            gate_up.append(pre_act)
            hidden.append((jax.nn.gelu(pre_act[:, :ff]) * pre_act[:, ff:]).astype(BF))

        grad_down = token_sum(c_half, hidden).astype(BF)
        down_piece = scatter_z(grad_down)
        low = []
        for c_part, pre_act in zip(c_half, gate_up):
            grad_hidden = dot(c_part, w_down_t, 1, 0)
            _, pull = jax.vjp(lambda a, b: jax.nn.gelu(a) * b, pre_act[:, :ff], pre_act[:, ff:])
            low.append(jnp.concatenate([(a + zero(grad_down)).astype(BF) for a in pull(grad_hidden)], axis=1))
        arrived = swap_core(dot(low[1], w_in, 1, 1, BF))
        sums = (dot(low[0], w_in, 1, 1) + arrived.astype(F32)).astype(BF)
        low_all = jnp.concatenate([a + zero(sums).astype(BF) for a in low], axis=0)
        grad_in = dot(jnp.concatenate(normed, axis=0), low_all, 0, 0).astype(BF)
        in_piece = scatter_z(grad_in)
        hidden = [a + zero(sums).astype(BF) for a in hidden]
        arrived = swap_core(dot(hidden[1], w_down_t, 1, 1, BF))
        result_sums = (dot(hidden[0], w_down_t, 1, 1) + arrived.astype(F32)).astype(BF)
        grad_normed = scatter4(sums) + zero(grad_in, down_piece, result_sums)
        _, pull = jax.vjp(rms_scale, after_mix, mlp_gain_f)
        grad_after, grad_mlp_gain = pull(grad_normed)
        grad_after = own_part(cotangent).astype(F32) + grad_after
        after_own = grad_after.astype(BF)
        after_near = gather4(after_own)
        after_low = [after_near, swap_core(after_near)]
        grad_mixed = [dot(a, w_out_t, 1, 0) for a in after_low]
        grad_out = token_sum(after_low, (mixed_near, mixed_far))
        grad_out = grad_out[:, :ch].astype(BF)

        out_piece = scatter_z(grad_out)
        mix_low, gate_low, acc = backward_call(
            mix, grad_mixed, mask, par_f, wg, values, pre, h_all, grad_out, result_sums
        )
        result = after_mix + scatter4(result_sums) + zero(mix_low)
        low_near, low_far = halves(mix_low)
        arrived = swap_core(dot(low_far, w_mix, 1, 1, BF))
        sums = (dot(low_near, w_mix, 1, 1) + arrived.astype(F32) + zero(result)).astype(BF)
        behind = zero(sums).astype(BF)
        first_sums = sums[:, : 2 * wide]
        nothing = (first_sums != first_sums).astype(BF)
        grad_mix = token_sum(normed_mix, (low_near + nothing, low_far + nothing))
        gate_low = gate_low + behind
        grad_mix = jnp.concatenate([grad_mix[:, :ch], grad_mix[:, wide : wide + ch]], axis=1).astype(BF)

        grad_gates = dot(values, gate_low, 0, 0)
        grad_gates = jnp.stack(
            [
                grad_gates[h * BW : (h + 1) * BW, q * wide + h * BW : q * wide + (h + 1) * BW]
                for q in range(2)
                for h in range(heads)
            ]
        )
        grad_gates = jnp.swapaxes(grad_gates.reshape(gate_rows, n, gate_width), 0, 1).reshape(n, -1)
        acc = jnp.sum(acc, axis=1)[:, :ch]
        chan_grad = jnp.concatenate(
            [acc[: taps + 2], acc[taps + 2 :] * (8.0 * jax.nn.sigmoid(-chan[taps + 2 :]))], axis=0
        )
        chan_grad = jnp.concatenate([jnp.where(g == j, chan_grad, 0.0) for j in range(G)], axis=1)
        chan_grad = jnp.transpose(chan_grad.reshape(taps + 3, n, part), (1, 0, 2)).reshape(n, -1)
        extra = jnp.concatenate([grad_gates, chan_grad, grad_mlp_gain.reshape(n, depth)], axis=1)
        more = -(-extra.shape[1] // (2 * ch))
        extra = jnp.pad(extra, ((0, 0), (0, more * 2 * ch - extra.shape[1]))).astype(BF)
        grad_mix = jnp.concatenate(
            [grad_mix.reshape(n, depth, -1), extra.reshape(n, more, 2 * ch)], axis=1
        )
        mix_piece = scatter_z(grad_mix)
        sums = trade(sums.reshape(G, row, -1))
        grad_normed_mix = jnp.sum(sums.astype(F32), axis=0) + zero(grad_mix, in_piece, out_piece)
        _, pull = jax.vjp(rms_scale, x_own_f, mixer_gain_f)
        grad_x, grad_mix_gain = pull(grad_normed_mix)
        input_grad_own = grad_after + grad_x

        pieces = [p.reshape(G, depth, -1) for p in (down_piece, in_piece, out_piece)]
        got = trade(jnp.concatenate(pieces, axis=2) + zero(sums).astype(BF))
        outs = []
        for at, size in ((0, ff), (ff, ff), (2 * ff, ff), (3 * ff, ch)):
            outs.append(jnp.swapaxes(got[:, :, at : at + size], 0, 1).reshape(depth, -1).astype(F32))
        out_down, out_gate, out_up, out_out = outs
        got = trade(mix_piece)
        out_branch, out_recur = [
            jnp.swapaxes(got[:, :depth, at : at + ch], 0, 1).reshape(depth, -1).astype(F32) for at in (0, ch)
        ]
        got = got[:, depth:].reshape(G, -1)
        gate_size = gate_rows * gate_width
        flat = jnp.swapaxes(got[:, :gate_size].reshape(G, 2, heads, -1), 0, 1)
        flat = flat.reshape(2, G * heads, -1).astype(F32)
        got = jnp.sum(got[:, gate_size : gate_size + (taps + 3) * part + depth].astype(F32), axis=0)
        chan_out = got[: (taps + 3) * part].reshape(taps + 3, part)
        mlp_gain_out = got[(taps + 3) * part :]
        mlp_gain_out = mlp_gain_out + swap_core(mlp_gain_out)
        def sum_flips(a, at, count, step):
            total = pick(a, at)
            for k in range(1, count):
                pairs = [(i, i ^ (k * step)) for i in range(n)]
                total = total + lax.ppermute(pick(a, at ^ k), "dp", pairs)
            return total

        mix_gain_out = sum_flips(grad_mix_gain.reshape(far, G, depth), dp // G, far, G)
        mix_gain_out = sum_flips(mix_gain_out, g, G, 1)
        mix_gain_out = mix_gain_out + swap_core(mix_gain_out)

        def both_rows(own):
            other = swap_core(own)
            first = jnp.where(mp == 0, own, other)
            second = jnp.where(mp == 0, other, own)
            return jnp.stack([first, second])[:, None]

        return (
            both_rows(result),
            both_rows(input_grad_own),
            mix_gain_out,
            mlp_gain_out,
            out_branch,
            out_recur,
            chan_out[:taps],
            flat[0],
            flat[1],
            chan_out[taps : taps + 2],
            chan_out[taps + 2],
            out_out.T,
            out_gate,
            out_up,
            out_down.T,
        )

    return body


def solution(mesh):
    in_specs = (
        P(None, "dp", None, None),
        P(None, "dp", None),
        P(None, "dp", None, None),
        P("dp"),
        P("dp"),
        P("dp", "mp"),
        P("dp", "mp"),
        P(None, ("mp", "dp")),
        P("mp", "dp"),
        P("mp", "dp"),
        P(None, ("mp", "dp")),
        P(("mp", "dp")),
        P("mp", "dp"),
        P("dp", "mp"),
        P("dp", "mp"),
        P("mp", "dp"),
    )
    out_specs = (
        P(None, "dp", None, None),
        P(None, "dp", None, None),
        P("dp"),
        P("dp"),
        P("dp", "mp"),
        P("dp", "mp"),
        P(None, ("mp", "dp")),
        P("mp", "dp"),
        P("mp", "dp"),
        P(None, ("mp", "dp")),
        P(("mp", "dp")),
        P("mp", "dp"),
        P("dp", "mp"),
        P("dp", "mp"),
        P("mp", "dp"),
    )
    body = make_body(mesh.shape["dp"], mesh.shape["mp"])
    return jax.shard_map(body, mesh=mesh, in_specs=in_specs, out_specs=out_specs, check_vma=False)
```

```python
import functools

import jax
import jax.numpy as jnp
from jax import lax
from jax.experimental import pallas as pl
from jax.experimental.pallas import tpu as pltpu
from jax.sharding import PartitionSpec as P

BW = 160
G = 4
BF = jnp.bfloat16
F32 = jnp.float32
ROWS = 8
HALF = ROWS // 2
PAD = 8
C0 = 0.7978845608028654
C1 = 0.044715


def sigmoid(v):
    return 0.5 * jnp.tanh(0.5 * v) + 0.5


def gates(dec, inp, sp8, keep):
    r = sigmoid(dec)
    i = sigmoid(inp)
    log_decay = r * sp8
    a = jnp.exp(log_decay)
    gap = -jnp.tanh(log_decay) * (1.0 + a * a)
    return r, i, a, gap


def forward_kernel(cp, row, unroll, extra, near_hbm, far_hbm, mask_ref, par_ref, wg_ref, *refs):
    mixed_ref, values_ref, pre_ref, h_ref, vals, mixf, mix, sems = refs[extra:]
    lanes = cp // 128
    order = list(range(lanes, 2 * lanes)) + list(range(lanes))
    copies = {
        j: [pltpu.make_async_copy((near_hbm, far_hbm)[r // HALF].at[pl.ds(r % HALF * row, row), pl.ds(128 * j, 128)], mix.at[j, pl.ds(r * (row + PAD), row)], sems.at[j, r]) for r in range(ROWS)] for j in order
    }
    for j in order:
        for c in copies[j]:
            c.start()

    def at(ref, t, off=0):
        return [ref[off + j, pl.ds(t, ROWS, stride=row + PAD), :] for j in range(lanes)]

    def put(ref, t, tiles):
        for j in range(lanes):
            ref[j, pl.ds(t, ROWS, stride=row + PAD), :] = tiles[j]

    def flat(ref, rows):
        return jnp.concatenate([ref[j, rows, :] for j in range(lanes)], axis=1)

    def mask(k, t):
        return mask_ref[k, pl.ds(pl.multiple_of(t * ROWS, ROWS), ROWS), :]

    par = [[par_ref[p, :, pl.ds(128 * j, 128)] for j in range(lanes)] for p in range(7)]
    zero = [jnp.zeros((ROWS, 128), F32)] * lanes
    for j in order[:lanes]:
        for c in copies[j]:
            c.wait()

    def conv_step(blk, carry):
        prev = [list(carry[0:lanes]), list(carry[lanes:2 * lanes]), list(carry[2 * lanes:])]
        for u in range(unroll):
            t = blk * unroll + u
            now = at(mix, t, lanes)
            same = [mask(k, t) for k in range(3)]
            out = []
            for j in range(lanes):
                s = now[j] * par[0][j]
                for k in range(3):
                    s = s + par[k + 1][j] * prev[k][j] * same[k]
                out.append(s)
            put(vals, t, out)
            prev = [now, prev[0], prev[1]]
        return tuple(prev[0] + prev[1] + prev[2])

    lax.fori_loop(0, row // unroll, conv_step, tuple(zero * 3))

    for r in range(ROWS):
        rows = pl.ds(r * row, row)
        prow = pl.ds(r * (row + PAD), row)
        low = flat(vals, prow).astype(BF)
        values_ref[rows, :] = low
        pre = jnp.dot(low, wg_ref[...], preferred_element_type=F32)
        for j in range(2 * lanes):
            pre_ref[j, prow, :] = pre[:, 128 * j : 128 * (j + 1)]
    for j in order[lanes:]:
        for c in copies[j]:
            c.wait()

    def step(blk, carry):
        h = list(carry)
        for u in range(unroll):
            t = blk * unroll + u
            dec, inp, val, br = at(pre_ref, t), at(pre_ref, t, lanes), at(vals, t), at(mix, t)
            keep = mask(0, t)
            out = []
            for j in range(lanes):
                r, i, a, gap = gates(dec[j] + par[4][j], inp[j] + par[5][j], par[6][j], keep)
                m = (1.0 - keep) + keep * jnp.sqrt(jnp.maximum(gap, 0.0))
                v = val[j].astype(BF).astype(F32)
                h[j] = a * keep * h[j] + m * i * v
                b = br[j]
                tt = jnp.tanh(C0 * (b + C1 * b * b * b))
                out.append(h[j] * (0.5 * b * (1.0 + tt)))
            put(h_ref, t, h)
            put(mixf, t, out)
        return tuple(h)

    lax.fori_loop(0, row // unroll, step, tuple(zero))
    for r in range(ROWS):
        rows = pl.ds(r * row, row)
        mixed_ref[rows, :] = flat(mixf, pl.ds(r * (row + PAD), row)).astype(BF)


def forward_call(near, far, mask, par, wg, *earlier, unroll=8):
    tokens, cp = 2 * near.shape[0], near.shape[1] // 2
    row = tokens // ROWS
    lanes = cp // 128
    vm = pl.BlockSpec(memory_space=pltpu.VMEM)
    hbm = pl.BlockSpec(memory_space=pl.ANY)
    return pl.pallas_call(
        functools.partial(forward_kernel, cp, row, unroll, len(earlier)),
        in_specs=[hbm] * 2 + [vm] * 3 + [hbm] * len(earlier),
        out_specs=(vm, vm, vm, vm),
        out_shape=(
            jax.ShapeDtypeStruct((tokens, cp), BF),
            jax.ShapeDtypeStruct((tokens, cp), BF),
            jax.ShapeDtypeStruct((2 * lanes, tokens + ROWS * PAD, 128), F32),
            jax.ShapeDtypeStruct((lanes, tokens + ROWS * PAD, 128), F32),
        ),
        scratch_shapes=[
            pltpu.VMEM((lanes, tokens + ROWS * PAD, 128), F32),
            pltpu.VMEM((lanes, tokens + ROWS * PAD, 128), F32),
            pltpu.VMEM((2 * lanes, tokens + ROWS * PAD, 128), F32),
            pltpu.SemaphoreType.DMA((2 * lanes, ROWS)),
        ],
        compiler_params=pltpu.CompilerParams(vmem_limit_bytes=36 * 1024 * 1024),
        cost_estimate=pl.CostEstimate(flops=150 * tokens * cp, bytes_accessed=84 * tokens * cp, transcendentals=6 * tokens * cp),
        name="recur_forward",
    )(near, far, mask, par, wg, *earlier)


def backward_kernel(
    cp, row, unroll, extra, mix_near, mix_far, gm_near, gm_far, mask_ref, par_ref, wg_ref, values_ref, pre_ref, h_ref,
    *refs,
):
    mixlow_ref, low_ref, acc_ref, vals, mix, gm, gdec, ginp, gval, sems = refs[extra:]
    lanes = cp // 128
    pitch = row + PAD
    copies = []
    for j in range(lanes):
        for r in range(ROWS):
            src = pl.ds(r % HALF * row, row)
            mix_hbm, gm_hbm = ((mix_near, gm_near), (mix_far, gm_far))[r // HALF]
            dst = pl.ds(r * pitch, row)
            cols = pl.ds(128 * j, 128)
            rec = pl.ds(cp + 128 * j, 128)
            copies.append(pltpu.make_async_copy(mix_hbm.at[src, cols], mix.at[j, dst], sems.at[0, j, r]))
            copies.append(
                pltpu.make_async_copy(mix_hbm.at[src, rec], mix.at[lanes + j, dst], sems.at[1, j, r])
            )
            copies.append(pltpu.make_async_copy(gm_hbm.at[src, cols], gm.at[j, dst], sems.at[2, j, r]))
    for c in copies:
        c.start()

    def at(ref, t, off=0):
        return [ref[off + j, pl.ds(t, ROWS, stride=pitch), :] for j in range(lanes)]

    def put(ref, t, tiles):
        for j in range(lanes):
            ref[j, pl.ds(t, ROWS, stride=pitch), :] = tiles[j]

    def flat(ref, rows):
        return jnp.concatenate([ref[j, rows, :] for j in range(lanes)], axis=1)

    def mask(k, t):
        return mask_ref[k, pl.ds(pl.multiple_of(t * ROWS, ROWS), ROWS), :]

    par = [[par_ref[p, :, pl.ds(128 * j, 128)] for j in range(lanes)] for p in range(7)]
    zero = [jnp.zeros((ROWS, 128), F32)] * lanes
    for r in range(ROWS):
        low = values_ref[pl.ds(r * row, row), :].astype(F32)
        for j in range(lanes):
            vals[j, pl.ds(r * pitch, row), :] = low[:, 128 * j : 128 * (j + 1)]
    for c in copies:
        c.wait()

    def step(blk, carry):
        carry = [list(carry[lanes * p : lanes * (p + 1)]) for p in range(4)]
        ag, sum_dec, sum_inp, sum_raw = carry
        for u in range(unroll):
            t = row - 1 - (blk * unroll + u)
            dec, inp, val = at(pre_ref, t), at(pre_ref, t, lanes), at(vals, t)
            br, up, here, before = at(mix, t), at(gm, t), at(h_ref, t), at(h_ref, jnp.maximum(t - 1, 0))
            keep = mask(0, t)
            out_b, out_d, out_i, out_v = [], [], [], []
            for j in range(lanes):
                r, i, a, gap = gates(dec[j] + par[4][j], inp[j] + par[5][j], par[6][j], keep)
                gap = jnp.maximum(gap, 1e-30)
                inv = lax.rsqrt(gap)
                m = (1.0 - keep) + keep * (gap * inv)
                b = br[j]
                sq = b * b
                tt = jnp.tanh(C0 * (b + C1 * b * sq))
                half = 0.5 * (1.0 + tt)
                slope = half + 0.5 * b * (1.0 - tt * tt) * (C0 + 3.0 * C0 * C1 * sq)
                g = up[j] * (b * half) + ag[j]
                gi = g * i
                decay = a * keep
                g_log = g * before[j] * decay - gi * val[j] * keep * (a * a * inv)
                ag[j] = decay * g
                gr = g_log * r
                g_dec = gr * par[6][j] * (1.0 - r)
                g_dir = gi * m
                g_inp = g_dir * val[j] * (1.0 - i)
                sum_raw[j] = sum_raw[j] + gr
                sum_dec[j] = sum_dec[j] + g_dec
                sum_inp[j] = sum_inp[j] + g_inp
                out_b.append(up[j] * here[j] * slope)
                out_d.append(g_dec)
                out_i.append(g_inp)
                out_v.append(g_dir)
            put(gm, t, out_b)
            put(gdec, t, out_d)
            put(ginp, t, out_i)
            put(gval, t, out_v)
        return tuple(ag + sum_dec + sum_inp + sum_raw)

    sums = lax.fori_loop(0, row // unroll, step, tuple(zero * 4))
    for p in range(3):
        for j in range(lanes):
            acc_ref[4 + p, :, pl.ds(128 * j, 128)] = sums[lanes * (p + 1) + j]

    for r in range(ROWS):
        rows = pl.ds(r * row, row)
        prow = pl.ds(r * pitch, row)
        low = jnp.concatenate([flat(gdec, prow), flat(ginp, prow)], axis=1).astype(BF)
        low_ref[rows, :] = low
        back = lax.dot_general(low, wg_ref[...], (((1,), (1,)), ((), ())), preferred_element_type=F32)
        for j in range(lanes):
            gval[j, prow, :] = gval[j, prow, :] + back[:, 128 * j : 128 * (j + 1)]
        mixlow_ref[rows, pl.ds(0, cp)] = flat(gm, prow).astype(BF)

    def conv_step(blk, carry):
        carry = [list(carry[lanes * p : lanes * (p + 1)]) for p in range(10)]
        late, sums = carry[:6], carry[6:]
        for u in range(unroll):
            t = row - 1 - (blk * unroll + u)
            now, rec = at(gval, t), at(mix, t, lanes)
            same = [mask(k, t) for k in range(3)]
            taps = [now, late[0], late[1], late[3]]
            out = []
            for j in range(lanes):
                s = par[0][j] * now[j]
                for k in range(1, 4):
                    s = s + par[k][j] * taps[k][j]
                out.append(s)
                for k in range(4):
                    sums[k][j] = sums[k][j] + rec[j] * taps[k][j]
            put(gdec, t, out)
            scaled = [[now[j] * same[k] for j in range(lanes)] for k in range(3)]
            late = [scaled[0], late[2], scaled[1], late[4], late[5], scaled[2]]
        return tuple(sum(late + sums, []))

    sums = lax.fori_loop(0, row // unroll, conv_step, tuple(zero * 10))
    for k in range(4):
        for j in range(lanes):
            acc_ref[k, :, pl.ds(128 * j, 128)] = sums[lanes * (6 + k) + j]
    for r in range(ROWS):
        mixlow_ref[pl.ds(r * row, row), pl.ds(cp, cp)] = flat(gdec, pl.ds(r * pitch, row)).astype(BF)


def backward_call(mix, gm, mask, par, wg, values, pre, h, *earlier, unroll=8):
    tokens, cp = 2 * gm[0].shape[0], gm[0].shape[1]
    row = tokens // ROWS
    lanes = cp // 128
    vm = pl.BlockSpec(memory_space=pltpu.VMEM)
    hbm = pl.BlockSpec(memory_space=pl.ANY)
    slab = pltpu.VMEM((lanes, tokens + ROWS * PAD, 128), F32)
    return pl.pallas_call(
        functools.partial(backward_kernel, cp, row, unroll, len(earlier)),
        in_specs=[hbm] * 4 + [vm] * 6 + [hbm] * len(earlier),
        out_specs=(vm, vm, vm),
        out_shape=(
            jax.ShapeDtypeStruct((tokens, 2 * cp), BF),
            jax.ShapeDtypeStruct((tokens, 2 * cp), BF),
            jax.ShapeDtypeStruct((7, ROWS, cp), F32),
        ),
        scratch_shapes=[
            slab,
            pltpu.VMEM((2 * lanes, tokens + ROWS * PAD, 128), F32),
            slab,
            slab,
            slab,
            slab,
            pltpu.SemaphoreType.DMA((3, lanes, ROWS)),
        ],
        compiler_params=pltpu.CompilerParams(vmem_limit_bytes=48 * 1024 * 1024),
        cost_estimate=pl.CostEstimate(flops=200 * tokens * cp, bytes_accessed=128 * tokens * cp, transcendentals=6 * tokens * cp),
        name="recur_backward",
    )(*mix, *gm, mask, par, wg, values, pre, h, *earlier)


def rms_scale(values, norm_gain):
    return values * lax.rsqrt(jnp.mean(values * values, axis=-1, keepdims=True) + 1e-06) * norm_gain


def same_masks(seg_rows, tap_count):
    same_seg = []
    for offset in range(1, tap_count):
        matched = (seg_rows[..., offset:] == seg_rows[..., :-offset]).astype(F32)
        leading = jnp.zeros(seg_rows.shape[:-1] + (offset,), F32)
        same_seg.append(jnp.concatenate([leading, matched], axis=-1))
    return jnp.stack(same_seg)


def dot(a, b, ca, cb, out=F32):
    return lax.dot_general(a, b, (((ca,), (cb,)), ((), ())), preferred_element_type=out)


def make_body(n, m):
    far = n // G
    planes = [[G * k + c for c in range(G)] for k in range(far)]
    lines = [[c + G * k for k in range(far)] for c in range(G)]
    cores = [(0, 1), (1, 0)]

    def trade(a, groups=planes):
        return lax.all_to_all(a, "dp", 0, 0, axis_index_groups=groups, tiled=True)

    def spread(a, groups=planes):
        return trade(jnp.broadcast_to(a, (len(groups[0]),) + a.shape), groups)

    def swap_core(a):
        return lax.ppermute(a, "mp", cores)

    def pick(a, i):
        return lax.dynamic_index_in_dim(a, i, 0, keepdims=False)

    def index_zero(*earlier):
        total = jnp.int32(0)
        for a in earlier:
            e = a[(0,) * a.ndim]
            total = total + (e != e).astype(jnp.int32)
        return total

    def zero(*earlier):
        return index_zero(*earlier).astype(F32)

    def body(
        inputs,
        segment_ids,
        cotangent,
        mixer_gain,
        mlp_gain,
        w_branch,
        w_recur,
        conv_w,
        w_decay,
        w_input,
        gate_bias,
        decay_param,
        w_out,
        w_gate,
        w_up,
        w_down,
    ):
        dp = lax.axis_index("dp")
        mp = lax.axis_index("mp")
        g = dp % G
        micro, _, row, width = inputs.shape
        depth = width // n
        ch = w_branch.shape[1] // G
        ff = w_gate.shape[1] // G
        heads = w_decay.shape[0] // G
        taps = conv_w.shape[0]
        part = conv_w.shape[1]
        wide = -(-ch // 128) * 128
        half = G * row

        def own_part(a, *earlier):
            return lax.dynamic_index_in_dim(a, mp + index_zero(*earlier), 0, keepdims=False)[0]

        def gather4(own):
            return spread(own).reshape(half, -1)

        def scatter4(sums):
            return jnp.sum(trade(sums.reshape(G, row, -1)).astype(F32), axis=0)

        def halves(a):
            return a[:half], a[half:]

        def token_sum(left, right):
            return dot(left[0], right[0], 0, 0) + dot(left[1], right[1], 0, 0)

        def scatter_z(grad):
            return lax.psum_scatter(grad, "dp", scatter_dimension=0, axis_index_groups=lines, tiled=True)

        def gather_z(rows):
            return lax.all_gather(rows, "dp", axis=0, axis_index_groups=lines, tiled=True)

        def by_column(weights):
            split = [jnp.swapaxes(w.reshape(depth, G, -1), 0, 1) for w in weights]
            return jnp.concatenate(split, axis=2)

        small = [a.reshape(-1) for a in (mixer_gain, mlp_gain, conv_w, gate_bias, decay_param)]
        small = jnp.concatenate(small + [segment_ids.astype(BF).reshape(-1)])
        small_size = small.shape[0] - micro * row
        gate_width = w_decay.shape[1]
        gate_rows = 2 * heads
        small_rows = -(-small.shape[0] // gate_width)
        small = jnp.pad(small, (0, small_rows * gate_width - small.shape[0]))
        pack = [w.reshape(G, heads * gate_width) for w in (w_decay, w_input)]
        pack = jnp.concatenate(pack + [jnp.broadcast_to(small, (G,) + small.shape)], axis=1)
        pack_size = pack.shape[1]
        first = by_column((w_branch, w_recur, w_out.T))
        columns = first.shape[2]
        pack_rows = -(-pack_size // columns)
        pack = jnp.pad(pack, ((0, 0), (0, pack_rows * columns - pack_size)))
        first = trade(jnp.concatenate([first, pack.reshape(G, pack_rows, columns)], axis=1))
        mix_rows = first[:, :depth].reshape(G * depth, -1)
        pack = first[:, depth:].reshape(G, -1)[:, :pack_size].reshape(G, gate_rows + small_rows, gate_width)
        seg_rows = pack[:, gate_rows:].reshape(G, -1)[:, small_size : small_size + micro * row]
        seg_rows = jnp.swapaxes(seg_rows.reshape(G, micro, row), 0, 1)
        seg_all = jnp.concatenate([pick(seg_rows, mp), pick(seg_rows, 1 - mp)], axis=0)
        packs = spread(pack, lines).reshape(n, gate_rows + small_rows, gate_width)
        small = packs[:, gate_rows:].reshape(n, -1)[:, :small_size].astype(F32)
        mixer_gain_f = small[:, :depth].reshape(width)
        mlp_gain_f = small[:, depth : 2 * depth].reshape(width)
        chan = small[:, 2 * depth :].reshape(n, taps + 3, part)
        chan = jnp.transpose(chan, (1, 0, 2)).reshape(taps + 3, n * part)
        chan = lax.dynamic_slice_in_dim(chan, g * ch, ch, 1)
        gates = packs[:, :gate_rows].reshape(n, 2, heads, -1)
        gates = jnp.transpose(gates, (1, 2, 0, 3)).reshape(2, heads, BW, BW)
        wg = [
            sum(
                jnp.pad(gates[q, h], ((h * BW, wide - (h + 1) * BW), (h * BW, wide - (h + 1) * BW)))
                for h in range(heads)
            )
            for q in range(2)
        ]
        wg = jnp.concatenate(wg, axis=1)
        sp8 = -8.0 * jax.nn.softplus(-chan[taps + 2 :])
        par = jnp.concatenate(
            [
                jnp.pad(chan[: taps + 2], ((0, 0), (0, wide - ch))),
                jnp.pad(sp8, ((0, 0), (0, wide - ch)), constant_values=-1.0),
            ],
            axis=0,
        )
        par_f = jnp.broadcast_to(par[:, None], (taps + 3, ROWS, wide))
        mask = jnp.transpose(same_masks(seg_all, taps), (0, 2, 1)).reshape(taps - 1, ROWS * row, 1)
        mask = jnp.broadcast_to(mask, (taps - 1, ROWS * row, 128))

        rows = gather_z(mix_rows)
        x_own_f = own_part(inputs).astype(F32)
        normed_own = rms_scale(x_own_f, mixer_gain_f)
        normed_near = gather4(normed_own.astype(BF))
        normed_mix = [normed_near, swap_core(normed_near)]
        w_in_rows = trade(by_column((w_gate, w_up))).reshape(G * depth, -1)
        w_down_rows = trade(by_column((w_down.T,))).reshape(G * depth, -1)
        w_down_t = gather_z(w_down_rows)
        c_near = gather4(own_part(cotangent, normed_near, w_down_rows))
        c_half = [c_near, swap_core(c_near)]
        w_in = gather_z(w_in_rows)
        w_mix = jnp.concatenate(
            [jnp.pad(w, ((0, 0), (0, wide - ch))) for w in (rows[:, :ch], rows[:, ch : 2 * ch])], axis=1
        ) + zero(w_in_rows).astype(BF)
        w_out_t = jnp.pad(rows[:, 2 * ch :], ((0, 0), (0, wide - ch)))

        mix = [dot(a, w_mix, 1, 0) for a in normed_mix]
        mixed, values, pre, h_all = forward_call(*mix, mask, par_f, wg)
        mixed_near, mixed_far = halves(mixed)
        c_part = c_near[:, :wide]
        mixed_far = mixed_far + (c_part != c_part).astype(BF)
        arrived = swap_core(dot(mixed_far, w_out_t, 1, 1, BF))
        sums = dot(mixed_near, w_out_t, 1, 1) + arrived.astype(F32)
        after_mix = x_own_f + scatter4(sums.astype(BF))
        normed_own = rms_scale(after_mix, mlp_gain_f).astype(BF)
        normed_near = gather4(normed_own)
        normed = [normed_near, swap_core(normed_near + zero(w_in).astype(BF))]
        hidden, gate_up = [], []
        for a in normed:
            pre_act = dot(a, w_in, 1, 0)
            gate_up.append(pre_act)
            act = jax.nn.gelu(pre_act[:, :ff]) * pre_act[:, ff:]
            hidden.append((act + zero(w_down_t) if hidden else act).astype(BF))

        grad_down = token_sum(c_half, hidden).astype(BF)
        down_piece = scatter_z(grad_down)
        low = []
        for c_part, pre_act in zip(c_half, gate_up):
            grad_hidden = dot(c_part, w_down_t, 1, 0)
            _, pull = jax.vjp(lambda a, b: jax.nn.gelu(a) * b, pre_act[:, :ff], pre_act[:, ff:])
            low.append(jnp.concatenate([(a + zero(grad_down)).astype(BF) for a in pull(grad_hidden)], axis=1))
        arrived = swap_core(dot(low[1], w_in, 1, 1, BF))
        sums = (dot(low[0], w_in, 1, 1) + arrived.astype(F32)).astype(BF)
        low_all = jnp.concatenate([a + zero(sums).astype(BF) for a in low], axis=0)
        grad_in = dot(jnp.concatenate(normed, axis=0), low_all, 0, 0).astype(BF)
        in_piece = scatter_z(grad_in)
        hidden = [a + zero(sums).astype(BF) for a in hidden]
        arrived = swap_core(dot(hidden[1], w_down_t, 1, 1, BF))
        result_sums = (dot(hidden[0], w_down_t, 1, 1) + arrived.astype(F32)).astype(BF)
        grad_normed = scatter4(sums) + zero(grad_in, down_piece, result_sums)
        _, pull = jax.vjp(rms_scale, after_mix, mlp_gain_f)
        grad_after, grad_mlp_gain = pull(grad_normed)
        grad_after = own_part(cotangent).astype(F32) + grad_after
        after_own = grad_after.astype(BF)
        after_near = gather4(after_own)
        after_low = [after_near, swap_core(after_near)]
        grad_mixed = [dot(a, w_out_t, 1, 0) for a in after_low]
        grad_out = token_sum(after_low, (mixed_near, mixed_far))
        grad_out = grad_out[:, :ch].astype(BF)

        out_piece = scatter_z(grad_out)
        mix_low, gate_low, acc = backward_call(
            mix, grad_mixed, mask, par_f, wg, values, pre, h_all, grad_out, result_sums
        )
        result = after_mix + scatter4(result_sums) + zero(mix_low)
        low_near, low_far = halves(mix_low)
        arrived = swap_core(dot(low_far, w_mix, 1, 1, BF))
        sums = (dot(low_near, w_mix, 1, 1) + arrived.astype(F32) + zero(result)).astype(BF)
        behind = zero(sums).astype(BF)
        first_sums = sums[:, : 2 * wide]
        nothing = (first_sums != first_sums).astype(BF)
        grad_mix = token_sum(normed_mix, (low_near + nothing, low_far + nothing))
        gate_low = gate_low + behind
        grad_mix = jnp.concatenate([grad_mix[:, :ch], grad_mix[:, wide : wide + ch]], axis=1).astype(BF)

        grad_gates = dot(values, gate_low, 0, 0)
        grad_gates = jnp.stack(
            [
                grad_gates[h * BW : (h + 1) * BW, q * wide + h * BW : q * wide + (h + 1) * BW]
                for q in range(2)
                for h in range(heads)
            ]
        )
        grad_gates = jnp.swapaxes(grad_gates.reshape(gate_rows, n, gate_width), 0, 1).reshape(n, -1)
        acc = jnp.sum(acc, axis=1)[:, :ch]
        chan_grad = jnp.concatenate(
            [acc[: taps + 2], acc[taps + 2 :] * (8.0 * jax.nn.sigmoid(-chan[taps + 2 :]))], axis=0
        )
        chan_grad = jnp.concatenate([jnp.where(g == j, chan_grad, 0.0) for j in range(G)], axis=1)
        chan_grad = jnp.transpose(chan_grad.reshape(taps + 3, n, part), (1, 0, 2)).reshape(n, -1)
        extra = jnp.concatenate([grad_gates, chan_grad, grad_mlp_gain.reshape(n, depth)], axis=1)
        more = -(-extra.shape[1] // (2 * ch))
        extra = jnp.pad(extra, ((0, 0), (0, more * 2 * ch - extra.shape[1]))).astype(BF)
        grad_mix = jnp.concatenate(
            [grad_mix.reshape(n, depth, -1), extra.reshape(n, more, 2 * ch)], axis=1
        )
        mix_piece = scatter_z(grad_mix)
        sums = trade(sums.reshape(G, row, -1))
        grad_normed_mix = jnp.sum(sums.astype(F32), axis=0) + zero(grad_mix, in_piece, out_piece)
        _, pull = jax.vjp(rms_scale, x_own_f, mixer_gain_f)
        grad_x, grad_mix_gain = pull(grad_normed_mix)
        input_grad_own = grad_after + grad_x

        pieces = [p.reshape(G, depth, -1) for p in (down_piece, in_piece, out_piece)]
        got = trade(jnp.concatenate(pieces, axis=2) + zero(sums).astype(BF))
        outs = []
        for at, size in ((0, ff), (ff, ff), (2 * ff, ff), (3 * ff, ch)):
            outs.append(jnp.swapaxes(got[:, :, at : at + size], 0, 1).reshape(depth, -1).astype(F32))
        out_down, out_gate, out_up, out_out = outs
        got = trade(mix_piece)
        out_branch, out_recur = [
            jnp.swapaxes(got[:, :depth, at : at + ch], 0, 1).reshape(depth, -1).astype(F32) for at in (0, ch)
        ]
        got = got[:, depth:].reshape(G, -1)
        gate_size = gate_rows * gate_width
        flat = jnp.swapaxes(got[:, :gate_size].reshape(G, 2, heads, -1), 0, 1)
        flat = flat.reshape(2, G * heads, -1).astype(F32)
        got = jnp.sum(got[:, gate_size : gate_size + (taps + 3) * part + depth].astype(F32), axis=0)
        chan_out = got[: (taps + 3) * part].reshape(taps + 3, part)
        mlp_gain_out = got[(taps + 3) * part :]
        mlp_gain_out = mlp_gain_out + swap_core(mlp_gain_out)
        def sum_flips(a, at, count, step):
            total = pick(a, at)
            for k in range(1, count):
                pairs = [(i, i ^ (k * step)) for i in range(n)]
                total = total + lax.ppermute(pick(a, at ^ k), "dp", pairs)
            return total

        mix_gain_out = sum_flips(grad_mix_gain.reshape(far, G, depth), dp // G, far, G)
        mix_gain_out = sum_flips(mix_gain_out, g, G, 1)
        mix_gain_out = mix_gain_out + swap_core(mix_gain_out)

        def both_rows(own):
            other = swap_core(own)
            first = jnp.where(mp == 0, own, other)
            second = jnp.where(mp == 0, other, own)
            return jnp.stack([first, second])[:, None]

        return (
            both_rows(result),
            both_rows(input_grad_own),
            mix_gain_out,
            mlp_gain_out,
            out_branch,
            out_recur,
            chan_out[:taps],
            flat[0],
            flat[1],
            chan_out[taps : taps + 2],
            chan_out[taps + 2],
            out_out.T,
            out_gate,
            out_up,
            out_down.T,
        )

    return body


def solution(mesh):
    in_specs = (
        P(None, "dp", None, None),
        P(None, "dp", None),
        P(None, "dp", None, None),
        P("dp"),
        P("dp"),
        P("dp", "mp"),
        P("dp", "mp"),
        P(None, ("mp", "dp")),
        P("mp", "dp"),
        P("mp", "dp"),
        P(None, ("mp", "dp")),
        P(("mp", "dp")),
        P("mp", "dp"),
        P("dp", "mp"),
        P("dp", "mp"),
        P("mp", "dp"),
    )
    out_specs = (
        P(None, "dp", None, None),
        P(None, "dp", None, None),
        P("dp"),
        P("dp"),
        P("dp", "mp"),
        P("dp", "mp"),
        P(None, ("mp", "dp")),
        P("mp", "dp"),
        P("mp", "dp"),
        P(None, ("mp", "dp")),
        P(("mp", "dp")),
        P("mp", "dp"),
        P("dp", "mp"),
        P("dp", "mp"),
        P("mp", "dp"),
    )
    body = make_body(mesh.shape["dp"], mesh.shape["mp"])
    return jax.shard_map(body, mesh=mesh, in_specs=in_specs, out_specs=out_specs, check_vma=False)
```

```python
import functools

import jax
import jax.numpy as jnp
from jax import lax
from jax.experimental import pallas as pl
from jax.experimental.pallas import tpu as pltpu
from jax.sharding import PartitionSpec as P

BW = 160
G = 4
BF = jnp.bfloat16
F32 = jnp.float32
ROWS = 8
HALF = ROWS // 2
PAD = 8
C0 = 0.7978845608028654
C1 = 0.044715


def sigmoid(v):
    return 0.5 * jnp.tanh(0.5 * v) + 0.5


def gates(dec, inp, sp8, keep):
    r = sigmoid(dec)
    i = sigmoid(inp)
    log_decay = r * sp8
    a = jnp.exp(log_decay)
    gap = -jnp.tanh(log_decay) * (1.0 + a * a)
    return r, i, a, gap


def forward_kernel(cp, row, unroll, extra, near_hbm, far_hbm, mask_ref, par_ref, wg_ref, *refs):
    mixed_ref, values_ref, pre_ref, h_ref, vals, mixf, mix, sems = refs[extra:]
    lanes = cp // 128
    order = list(range(lanes, 2 * lanes)) + list(range(lanes))
    copies = {
        j: [pltpu.make_async_copy((near_hbm, far_hbm)[r // HALF].at[pl.ds(r % HALF * row, row), pl.ds(128 * j, 128)], mix.at[j, pl.ds(r * (row + PAD), row)], sems.at[j, r]) for r in range(ROWS)] for j in order
    }
    for j in order:
        for c in copies[j]:
            c.start()

    def at(ref, t, off=0):
        return [ref[off + j, pl.ds(t, ROWS, stride=row + PAD), :] for j in range(lanes)]

    def put(ref, t, tiles):
        for j in range(lanes):
            ref[j, pl.ds(t, ROWS, stride=row + PAD), :] = tiles[j]

    def flat(ref, rows):
        return jnp.concatenate([ref[j, rows, :] for j in range(lanes)], axis=1)

    def mask(k, t):
        return mask_ref[k, pl.ds(pl.multiple_of(t * ROWS, ROWS), ROWS), :]

    par = [[par_ref[p, :, pl.ds(128 * j, 128)] for j in range(lanes)] for p in range(7)]
    zero = [jnp.zeros((ROWS, 128), F32)] * lanes
    for j in order[:lanes]:
        for c in copies[j]:
            c.wait()

    def conv_step(blk, carry):
        prev = [list(carry[0:lanes]), list(carry[lanes:2 * lanes]), list(carry[2 * lanes:])]
        for u in range(unroll):
            t = blk * unroll + u
            now = at(mix, t, lanes)
            same = [mask(k, t) for k in range(3)]
            out = []
            for j in range(lanes):
                s = now[j] * par[0][j]
                for k in range(3):
                    s = s + par[k + 1][j] * prev[k][j] * same[k]
                out.append(s)
            put(vals, t, out)
            prev = [now, prev[0], prev[1]]
        return tuple(prev[0] + prev[1] + prev[2])

    lax.fori_loop(0, row // unroll, conv_step, tuple(zero * 3))

    for r in range(ROWS):
        rows = pl.ds(r * row, row)
        prow = pl.ds(r * (row + PAD), row)
        low = flat(vals, prow).astype(BF)
        values_ref[rows, :] = low
        pre = jnp.dot(low, wg_ref[...], preferred_element_type=F32)
        for j in range(2 * lanes):
            pre_ref[j, prow, :] = pre[:, 128 * j : 128 * (j + 1)]
    for j in order[lanes:]:
        for c in copies[j]:
            c.wait()

    def step(blk, carry):
        h = list(carry)
        for u in range(unroll):
            t = blk * unroll + u
            dec, inp, val, br = at(pre_ref, t), at(pre_ref, t, lanes), at(vals, t), at(mix, t)
            keep = mask(0, t)
            out = []
            for j in range(lanes):
                r, i, a, gap = gates(dec[j] + par[4][j], inp[j] + par[5][j], par[6][j], keep)
                m = (1.0 - keep) + keep * jnp.sqrt(jnp.maximum(gap, 0.0))
                v = val[j].astype(BF).astype(F32)
                h[j] = a * keep * h[j] + m * i * v
                b = br[j]
                tt = jnp.tanh(C0 * (b + C1 * b * b * b))
                out.append(h[j] * (0.5 * b * (1.0 + tt)))
            put(h_ref, t, h)
            put(mixf, t, out)
        return tuple(h)

    lax.fori_loop(0, row // unroll, step, tuple(zero))
    for r in range(ROWS):
        rows = pl.ds(r * row, row)
        mixed_ref[rows, :] = flat(mixf, pl.ds(r * (row + PAD), row)).astype(BF)


def forward_call(near, far, mask, par, wg, *earlier, unroll=8):
    tokens, cp = 2 * near.shape[0], near.shape[1] // 2
    row = tokens // ROWS
    lanes = cp // 128
    vm = pl.BlockSpec(memory_space=pltpu.VMEM)
    hbm = pl.BlockSpec(memory_space=pl.ANY)
    return pl.pallas_call(
        functools.partial(forward_kernel, cp, row, unroll, len(earlier)),
        in_specs=[hbm] * 2 + [vm] * 3 + [hbm] * len(earlier),
        out_specs=(vm, vm, vm, vm),
        out_shape=(
            jax.ShapeDtypeStruct((tokens, cp), BF),
            jax.ShapeDtypeStruct((tokens, cp), BF),
            jax.ShapeDtypeStruct((2 * lanes, tokens + ROWS * PAD, 128), F32),
            jax.ShapeDtypeStruct((lanes, tokens + ROWS * PAD, 128), F32),
        ),
        scratch_shapes=[
            pltpu.VMEM((lanes, tokens + ROWS * PAD, 128), F32),
            pltpu.VMEM((lanes, tokens + ROWS * PAD, 128), F32),
            pltpu.VMEM((2 * lanes, tokens + ROWS * PAD, 128), F32),
            pltpu.SemaphoreType.DMA((2 * lanes, ROWS)),
        ],
        compiler_params=pltpu.CompilerParams(vmem_limit_bytes=36 * 1024 * 1024),
        cost_estimate=pl.CostEstimate(flops=150 * tokens * cp, bytes_accessed=84 * tokens * cp, transcendentals=6 * tokens * cp),
        name="recur_forward",
    )(near, far, mask, par, wg, *earlier)


def backward_kernel(
    cp, row, unroll, extra, mix_near, mix_far, gm_near, gm_far, mask_ref, par_ref, wg_ref, values_ref, pre_ref, h_ref,
    *refs,
):
    mixlow_ref, low_ref, acc_ref, vals, mix, gm, gdec, ginp, gval, sems = refs[extra:]
    lanes = cp // 128
    pitch = row + PAD
    copies = []
    for j in range(lanes):
        for r in range(ROWS):
            src = pl.ds(r % HALF * row, row)
            mix_hbm, gm_hbm = ((mix_near, gm_near), (mix_far, gm_far))[r // HALF]
            dst = pl.ds(r * pitch, row)
            cols = pl.ds(128 * j, 128)
            rec = pl.ds(cp + 128 * j, 128)
            copies.append(pltpu.make_async_copy(mix_hbm.at[src, cols], mix.at[j, dst], sems.at[0, j, r]))
            copies.append(
                pltpu.make_async_copy(mix_hbm.at[src, rec], mix.at[lanes + j, dst], sems.at[1, j, r])
            )
            copies.append(pltpu.make_async_copy(gm_hbm.at[src, cols], gm.at[j, dst], sems.at[2, j, r]))
    for c in copies:
        c.start()

    def at(ref, t, off=0):
        return [ref[off + j, pl.ds(t, ROWS, stride=pitch), :] for j in range(lanes)]

    def put(ref, t, tiles):
        for j in range(lanes):
            ref[j, pl.ds(t, ROWS, stride=pitch), :] = tiles[j]

    def flat(ref, rows):
        return jnp.concatenate([ref[j, rows, :] for j in range(lanes)], axis=1)

    def mask(k, t):
        return mask_ref[k, pl.ds(pl.multiple_of(t * ROWS, ROWS), ROWS), :]

    par = [[par_ref[p, :, pl.ds(128 * j, 128)] for j in range(lanes)] for p in range(7)]
    zero = [jnp.zeros((ROWS, 128), F32)] * lanes
    for r in range(ROWS):
        low = values_ref[pl.ds(r * row, row), :].astype(F32)
        for j in range(lanes):
            vals[j, pl.ds(r * pitch, row), :] = low[:, 128 * j : 128 * (j + 1)]
    for c in copies:
        c.wait()

    def step(blk, carry):
        carry = [list(carry[lanes * p : lanes * (p + 1)]) for p in range(4)]
        ag, sum_dec, sum_inp, sum_raw = carry
        for u in range(unroll):
            t = row - 1 - (blk * unroll + u)
            dec, inp, val = at(pre_ref, t), at(pre_ref, t, lanes), at(vals, t)
            br, up, here, before = at(mix, t), at(gm, t), at(h_ref, t), at(h_ref, jnp.maximum(t - 1, 0))
            keep = mask(0, t)
            out_b, out_d, out_i, out_v = [], [], [], []
            for j in range(lanes):
                r, i, a, gap = gates(dec[j] + par[4][j], inp[j] + par[5][j], par[6][j], keep)
                gap = jnp.maximum(gap, 1e-30)
                inv = lax.rsqrt(gap)
                m = (1.0 - keep) + keep * (gap * inv)
                b = br[j]
                sq = b * b
                tt = jnp.tanh(C0 * (b + C1 * b * sq))
                half = 0.5 * (1.0 + tt)
                slope = half + 0.5 * b * (1.0 - tt * tt) * (C0 + 3.0 * C0 * C1 * sq)
                g = up[j] * (b * half) + ag[j]
                gi = g * i
                decay = a * keep
                g_log = g * before[j] * decay - gi * val[j] * keep * (a * a * inv)
                ag[j] = decay * g
                gr = g_log * r
                g_dec = gr * par[6][j] * (1.0 - r)
                g_dir = gi * m
                g_inp = g_dir * val[j] * (1.0 - i)
                sum_raw[j] = sum_raw[j] + gr
                sum_dec[j] = sum_dec[j] + g_dec
                sum_inp[j] = sum_inp[j] + g_inp
                out_b.append(up[j] * here[j] * slope)
                out_d.append(g_dec)
                out_i.append(g_inp)
                out_v.append(g_dir)
            put(gm, t, out_b)
            put(gdec, t, out_d)
            put(ginp, t, out_i)
            put(gval, t, out_v)
        return tuple(ag + sum_dec + sum_inp + sum_raw)

    sums = lax.fori_loop(0, row // unroll, step, tuple(zero * 4))
    for p in range(3):
        for j in range(lanes):
            acc_ref[4 + p, :, pl.ds(128 * j, 128)] = sums[lanes * (p + 1) + j]

    for r in range(ROWS):
        rows = pl.ds(r * row, row)
        prow = pl.ds(r * pitch, row)
        low = jnp.concatenate([flat(gdec, prow), flat(ginp, prow)], axis=1).astype(BF)
        low_ref[rows, :] = low
        back = lax.dot_general(low, wg_ref[...], (((1,), (1,)), ((), ())), preferred_element_type=F32)
        for j in range(lanes):
            gval[j, prow, :] = gval[j, prow, :] + back[:, 128 * j : 128 * (j + 1)]
        mixlow_ref[rows, pl.ds(0, cp)] = flat(gm, prow).astype(BF)

    def conv_step(blk, carry):
        carry = [list(carry[lanes * p : lanes * (p + 1)]) for p in range(10)]
        late, sums = carry[:6], carry[6:]
        for u in range(unroll):
            t = row - 1 - (blk * unroll + u)
            now, rec = at(gval, t), at(mix, t, lanes)
            same = [mask(k, t) for k in range(3)]
            taps = [now, late[0], late[1], late[3]]
            out = []
            for j in range(lanes):
                s = par[0][j] * now[j]
                for k in range(1, 4):
                    s = s + par[k][j] * taps[k][j]
                out.append(s)
                for k in range(4):
                    sums[k][j] = sums[k][j] + rec[j] * taps[k][j]
            put(gdec, t, out)
            scaled = [[now[j] * same[k] for j in range(lanes)] for k in range(3)]
            late = [scaled[0], late[2], scaled[1], late[4], late[5], scaled[2]]
        return tuple(sum(late + sums, []))

    sums = lax.fori_loop(0, row // unroll, conv_step, tuple(zero * 10))
    for k in range(4):
        for j in range(lanes):
            acc_ref[k, :, pl.ds(128 * j, 128)] = sums[lanes * (6 + k) + j]
    for r in range(ROWS):
        mixlow_ref[pl.ds(r * row, row), pl.ds(cp, cp)] = flat(gdec, pl.ds(r * pitch, row)).astype(BF)


def backward_call(mix, gm, mask, par, wg, values, pre, h, *earlier, unroll=8):
    tokens, cp = 2 * gm[0].shape[0], gm[0].shape[1]
    row = tokens // ROWS
    lanes = cp // 128
    vm = pl.BlockSpec(memory_space=pltpu.VMEM)
    hbm = pl.BlockSpec(memory_space=pl.ANY)
    slab = pltpu.VMEM((lanes, tokens + ROWS * PAD, 128), F32)
    return pl.pallas_call(
        functools.partial(backward_kernel, cp, row, unroll, len(earlier)),
        in_specs=[hbm] * 4 + [vm] * 6 + [hbm] * len(earlier),
        out_specs=(vm, vm, vm),
        out_shape=(
            jax.ShapeDtypeStruct((tokens, 2 * cp), BF),
            jax.ShapeDtypeStruct((tokens, 2 * cp), BF),
            jax.ShapeDtypeStruct((7, ROWS, cp), F32),
        ),
        scratch_shapes=[
            slab,
            pltpu.VMEM((2 * lanes, tokens + ROWS * PAD, 128), F32),
            slab,
            slab,
            slab,
            slab,
            pltpu.SemaphoreType.DMA((3, lanes, ROWS)),
        ],
        compiler_params=pltpu.CompilerParams(vmem_limit_bytes=48 * 1024 * 1024),
        cost_estimate=pl.CostEstimate(flops=200 * tokens * cp, bytes_accessed=128 * tokens * cp, transcendentals=6 * tokens * cp),
        name="recur_backward",
    )(*mix, *gm, mask, par, wg, values, pre, h, *earlier)


def rms_scale(values, norm_gain):
    return values * lax.rsqrt(jnp.mean(values * values, axis=-1, keepdims=True) + 1e-06) * norm_gain


def same_masks(seg_rows, tap_count):
    same_seg = []
    for offset in range(1, tap_count):
        matched = (seg_rows[..., offset:] == seg_rows[..., :-offset]).astype(F32)
        leading = jnp.zeros(seg_rows.shape[:-1] + (offset,), F32)
        same_seg.append(jnp.concatenate([leading, matched], axis=-1))
    return jnp.stack(same_seg)


def dot(a, b, ca, cb, out=F32):
    return lax.dot_general(a, b, (((ca,), (cb,)), ((), ())), preferred_element_type=out)


def make_body(n, m):
    far = n // G
    planes = [[G * k + c for c in range(G)] for k in range(far)]
    lines = [[c + G * k for k in range(far)] for c in range(G)]
    cores = [(0, 1), (1, 0)]

    def trade(a, groups=planes):
        return lax.all_to_all(a, "dp", 0, 0, axis_index_groups=groups, tiled=True)

    def spread(a, groups=planes):
        return trade(jnp.broadcast_to(a, (len(groups[0]),) + a.shape), groups)

    def swap_core(a):
        return lax.ppermute(a, "mp", cores)

    def pick(a, i):
        return lax.dynamic_index_in_dim(a, i, 0, keepdims=False)

    def index_zero(*earlier):
        total = jnp.int32(0)
        for a in earlier:
            e = a[(0,) * a.ndim]
            total = total + (e != e).astype(jnp.int32)
        return total

    def zero(*earlier):
        return index_zero(*earlier).astype(F32)

    def body(
        inputs,
        segment_ids,
        cotangent,
        mixer_gain,
        mlp_gain,
        w_branch,
        w_recur,
        conv_w,
        w_decay,
        w_input,
        gate_bias,
        decay_param,
        w_out,
        w_gate,
        w_up,
        w_down,
    ):
        dp = lax.axis_index("dp")
        mp = lax.axis_index("mp")
        g = dp % G
        micro, _, row, width = inputs.shape
        depth = width // n
        ch = w_branch.shape[1] // G
        ff = w_gate.shape[1] // G
        heads = w_decay.shape[0] // G
        taps = conv_w.shape[0]
        part = conv_w.shape[1]
        wide = -(-ch // 128) * 128
        half = G * row

        def own_part(a, *earlier):
            return lax.dynamic_index_in_dim(a, mp + index_zero(*earlier), 0, keepdims=False)[0]

        def gather4(own):
            return spread(own).reshape(half, -1)

        def scatter4(sums):
            return jnp.sum(trade(sums.reshape(G, row, -1)).astype(F32), axis=0)

        def halves(a):
            return a[:half], a[half:]

        def token_sum(left, right):
            return dot(left[0], right[0], 0, 0) + dot(left[1], right[1], 0, 0)

        def scatter_z(grad):
            return lax.psum_scatter(grad, "dp", scatter_dimension=0, axis_index_groups=lines, tiled=True)

        def gather_z(rows):
            return lax.all_gather(rows, "dp", axis=0, axis_index_groups=lines, tiled=True)

        def by_column(weights):
            split = [jnp.swapaxes(w.reshape(depth, G, -1), 0, 1) for w in weights]
            return jnp.concatenate(split, axis=2)

        small = [a.reshape(-1) for a in (mixer_gain, mlp_gain, conv_w, gate_bias, decay_param)]
        small = jnp.concatenate(small + [segment_ids.astype(BF).reshape(-1)])
        small_size = small.shape[0] - micro * row
        gate_width = w_decay.shape[1]
        gate_rows = 2 * heads
        small_rows = -(-small.shape[0] // gate_width)
        small = jnp.pad(small, (0, small_rows * gate_width - small.shape[0]))
        pack = [w.reshape(G, heads * gate_width) for w in (w_decay, w_input)]
        pack = jnp.concatenate(pack + [jnp.broadcast_to(small, (G,) + small.shape)], axis=1)
        pack_size = pack.shape[1]
        first = by_column((w_branch, w_recur, w_out.T))
        columns = first.shape[2]
        pack_rows = -(-pack_size // columns)
        pack = jnp.pad(pack, ((0, 0), (0, pack_rows * columns - pack_size)))
        first = trade(jnp.concatenate([first, pack.reshape(G, pack_rows, columns)], axis=1))
        mix_rows = first[:, :depth].reshape(G * depth, -1)
        pack = first[:, depth:].reshape(G, -1)[:, :pack_size].reshape(G, gate_rows + small_rows, gate_width)
        seg_rows = pack[:, gate_rows:].reshape(G, -1)[:, small_size : small_size + micro * row]
        seg_rows = jnp.swapaxes(seg_rows.reshape(G, micro, row), 0, 1)
        seg_all = jnp.concatenate([pick(seg_rows, mp), pick(seg_rows, 1 - mp)], axis=0)
        packs = spread(pack, lines).reshape(n, gate_rows + small_rows, gate_width)
        small = packs[:, gate_rows:].reshape(n, -1)[:, :small_size].astype(F32)
        mixer_gain_f = small[:, :depth].reshape(width)
        mlp_gain_f = small[:, depth : 2 * depth].reshape(width)
        chan = small[:, 2 * depth :].reshape(n, taps + 3, part)
        chan = jnp.transpose(chan, (1, 0, 2)).reshape(taps + 3, n * part)
        chan = lax.dynamic_slice_in_dim(chan, g * ch, ch, 1)
        gates = packs[:, :gate_rows].reshape(n, 2, heads, -1)
        gates = jnp.transpose(gates, (1, 2, 0, 3)).reshape(2, heads, BW, BW)
        wg = [
            sum(
                jnp.pad(gates[q, h], ((h * BW, wide - (h + 1) * BW), (h * BW, wide - (h + 1) * BW)))
                for h in range(heads)
            )
            for q in range(2)
        ]
        wg = jnp.concatenate(wg, axis=1)
        sp8 = -8.0 * jax.nn.softplus(-chan[taps + 2 :])
        par = jnp.concatenate(
            [
                jnp.pad(chan[: taps + 2], ((0, 0), (0, wide - ch))),
                jnp.pad(sp8, ((0, 0), (0, wide - ch)), constant_values=-1.0),
            ],
            axis=0,
        )
        par_f = jnp.broadcast_to(par[:, None], (taps + 3, ROWS, wide))
        mask = jnp.transpose(same_masks(seg_all, taps), (0, 2, 1)).reshape(taps - 1, ROWS * row, 1)
        mask = jnp.broadcast_to(mask, (taps - 1, ROWS * row, 128))

        rows = gather_z(mix_rows)
        x_own_f = own_part(inputs).astype(F32)
        normed_own = rms_scale(x_own_f, mixer_gain_f)
        normed_near = gather4(normed_own.astype(BF))
        normed_mix = [normed_near, swap_core(normed_near)]
        w_in_rows = trade(by_column((w_gate, w_up))).reshape(G * depth, -1)
        w_down_rows = trade(by_column((w_down.T,))).reshape(G * depth, -1)
        w_down_t = gather_z(w_down_rows)
        c_near = gather4(own_part(cotangent, normed_near, w_down_rows))
        c_half = [c_near, swap_core(c_near)]
        w_in = gather_z(w_in_rows)
        w_mix = jnp.concatenate(
            [jnp.pad(w, ((0, 0), (0, wide - ch))) for w in (rows[:, :ch], rows[:, ch : 2 * ch])], axis=1
        ) + zero(w_in_rows).astype(BF)
        w_out_t = jnp.pad(rows[:, 2 * ch :], ((0, 0), (0, wide - ch)))

        mix = [dot(a, w_mix, 1, 0) for a in normed_mix]
        mixed, values, pre, h_all = forward_call(*mix, mask, par_f, wg)
        mixed_near, mixed_far = halves(mixed)
        c_part = c_near[:, :wide]
        mixed_far = mixed_far + (c_part != c_part).astype(BF)
        arrived = swap_core(dot(mixed_far, w_out_t, 1, 1, BF))
        sums = dot(mixed_near, w_out_t, 1, 1) + arrived.astype(F32)
        after_mix = x_own_f + scatter4(sums.astype(BF))
        normed_own = rms_scale(after_mix, mlp_gain_f).astype(BF)
        normed_near = gather4(normed_own)
        normed = [normed_near, swap_core(normed_near + zero(w_in).astype(BF))]
        hidden, gate_up = [], []
        for a in normed:
            pre_act = dot(a, w_in, 1, 0)
            gate_up.append(pre_act)
            act = jax.nn.gelu(pre_act[:, :ff]) * pre_act[:, ff:]
            hidden.append((act + zero(w_down_t) if hidden else act).astype(BF))

        grad_down = token_sum(c_half, hidden).astype(BF)
        down_piece = scatter_z(grad_down)
        low = []
        for c_part, pre_act in zip(c_half, gate_up):
            grad_hidden = dot(c_part, w_down_t, 1, 0)
            _, pull = jax.vjp(lambda a, b: jax.nn.gelu(a) * b, pre_act[:, :ff], pre_act[:, ff:])
            low.append(jnp.concatenate([(a + zero(grad_down)).astype(BF) for a in pull(grad_hidden)], axis=1))
        arrived = swap_core(dot(low[1], w_in, 1, 1, BF))
        sums = (dot(low[0], w_in, 1, 1) + arrived.astype(F32)).astype(BF)
        low_all = jnp.concatenate([a + zero(sums).astype(BF) for a in low], axis=0)
        grad_in = dot(jnp.concatenate(normed, axis=0), low_all, 0, 0).astype(BF)
        in_piece = scatter_z(grad_in)
        hidden = [a + zero(sums).astype(BF) for a in hidden]
        arrived = swap_core(dot(hidden[1], w_down_t, 1, 1, BF))
        result_sums = (dot(hidden[0], w_down_t, 1, 1) + arrived.astype(F32)).astype(BF)
        grad_normed = scatter4(sums) + zero(grad_in, down_piece, result_sums)
        _, pull = jax.vjp(rms_scale, after_mix, mlp_gain_f)
        grad_after, grad_mlp_gain = pull(grad_normed)
        grad_after = own_part(cotangent).astype(F32) + grad_after
        after_own = grad_after.astype(BF)
        after_near = gather4(after_own)
        after_low = [after_near, swap_core(after_near)]
        grad_mixed = [dot(a, w_out_t, 1, 0) for a in after_low]
        grad_out = token_sum(after_low, (mixed_near, mixed_far))
        grad_out = grad_out[:, :ch].astype(BF)

        out_piece = scatter_z(grad_out)
        mix_low, gate_low, acc = backward_call(
            mix, grad_mixed, mask, par_f, wg, values, pre, h_all, grad_out, result_sums
        )
        result = after_mix + scatter4(result_sums) + zero(mix_low)
        low_near, low_far = halves(mix_low)
        arrived = swap_core(dot(low_far, w_mix, 1, 1, BF))
        sums = (dot(low_near, w_mix, 1, 1) + arrived.astype(F32) + zero(result)).astype(BF)
        behind = zero(sums).astype(BF)
        first_sums = sums[:, : 2 * wide]
        nothing = (first_sums != first_sums).astype(BF)
        grad_mix = token_sum(normed_mix, (low_near + nothing, low_far + nothing))
        gate_low = gate_low + behind
        grad_mix = jnp.concatenate([grad_mix[:, :ch], grad_mix[:, wide : wide + ch]], axis=1).astype(BF)

        grad_gates = dot(values, gate_low, 0, 0)
        grad_gates = jnp.stack(
            [
                grad_gates[h * BW : (h + 1) * BW, q * wide + h * BW : q * wide + (h + 1) * BW]
                for q in range(2)
                for h in range(heads)
            ]
        )
        grad_gates = jnp.swapaxes(grad_gates.reshape(gate_rows, n, gate_width), 0, 1).reshape(n, -1)
        acc = jnp.sum(acc, axis=1)[:, :ch]
        chan_grad = jnp.concatenate(
            [acc[: taps + 2], acc[taps + 2 :] * (8.0 * jax.nn.sigmoid(-chan[taps + 2 :]))], axis=0
        )
        chan_grad = jnp.concatenate([jnp.where(g == j, chan_grad, 0.0) for j in range(G)], axis=1)
        chan_grad = jnp.transpose(chan_grad.reshape(taps + 3, n, part), (1, 0, 2)).reshape(n, -1)
        extra = jnp.concatenate([grad_gates, chan_grad, grad_mlp_gain.reshape(n, depth)], axis=1)
        more = -(-extra.shape[1] // (2 * ch))
        extra = jnp.pad(extra, ((0, 0), (0, more * 2 * ch - extra.shape[1]))).astype(BF)
        grad_mix = jnp.concatenate(
            [grad_mix.reshape(n, depth, -1), extra.reshape(n, more, 2 * ch)], axis=1
        )
        mix_piece = scatter_z(grad_mix)
        sums = trade(sums.reshape(G, row, -1))
        grad_normed_mix = jnp.sum(sums.astype(F32), axis=0) + zero(grad_mix, in_piece, out_piece)
        _, pull = jax.vjp(rms_scale, x_own_f, mixer_gain_f)
        grad_x, grad_mix_gain = pull(grad_normed_mix)
        input_grad_own = grad_after + grad_x

        pieces = [p.reshape(G, depth, -1) for p in (down_piece, in_piece, out_piece)]
        arrived = sums[:, :depth, :ff]
        pieces[0] = pieces[0] + (arrived != arrived).astype(BF)
        got = trade(jnp.concatenate(pieces, axis=2))
        outs = []
        for at, size in ((0, ff), (ff, ff), (2 * ff, ff), (3 * ff, ch)):
            outs.append(jnp.swapaxes(got[:, :, at : at + size], 0, 1).reshape(depth, -1).astype(F32))
        out_down, out_gate, out_up, out_out = outs
        got = trade(mix_piece)
        out_branch, out_recur = [
            jnp.swapaxes(got[:, :depth, at : at + ch], 0, 1).reshape(depth, -1).astype(F32) for at in (0, ch)
        ]
        got = got[:, depth:].reshape(G, -1)
        gate_size = gate_rows * gate_width
        flat = jnp.swapaxes(got[:, :gate_size].reshape(G, 2, heads, -1), 0, 1)
        flat = flat.reshape(2, G * heads, -1).astype(F32)
        got = jnp.sum(got[:, gate_size : gate_size + (taps + 3) * part + depth].astype(F32), axis=0)
        chan_out = got[: (taps + 3) * part].reshape(taps + 3, part)
        mlp_gain_out = got[(taps + 3) * part :]
        mlp_gain_out = mlp_gain_out + swap_core(mlp_gain_out)
        def sum_flips(a, at, count, step):
            total = pick(a, at)
            for k in range(1, count):
                pairs = [(i, i ^ (k * step)) for i in range(n)]
                total = total + lax.ppermute(pick(a, at ^ k), "dp", pairs)
            return total

        mix_gain_out = sum_flips(grad_mix_gain.reshape(far, G, depth), dp // G, far, G)
        mix_gain_out = sum_flips(mix_gain_out, g, G, 1)
        mix_gain_out = mix_gain_out + swap_core(mix_gain_out)

        def both_rows(own):
            other = swap_core(own)
            first = jnp.where(mp == 0, own, other)
            second = jnp.where(mp == 0, other, own)
            return jnp.stack([first, second])[:, None]

        return (
            both_rows(result),
            both_rows(input_grad_own),
            mix_gain_out,
            mlp_gain_out,
            out_branch,
            out_recur,
            chan_out[:taps],
            flat[0],
            flat[1],
            chan_out[taps : taps + 2],
            chan_out[taps + 2],
            out_out.T,
            out_gate,
            out_up,
            out_down.T,
        )

    return body


def solution(mesh):
    in_specs = (
        P(None, "dp", None, None),
        P(None, "dp", None),
        P(None, "dp", None, None),
        P("dp"),
        P("dp"),
        P("dp", "mp"),
        P("dp", "mp"),
        P(None, ("mp", "dp")),
        P("mp", "dp"),
        P("mp", "dp"),
        P(None, ("mp", "dp")),
        P(("mp", "dp")),
        P("mp", "dp"),
        P("dp", "mp"),
        P("dp", "mp"),
        P("mp", "dp"),
    )
    out_specs = (
        P(None, "dp", None, None),
        P(None, "dp", None, None),
        P("dp"),
        P("dp"),
        P("dp", "mp"),
        P("dp", "mp"),
        P(None, ("mp", "dp")),
        P("mp", "dp"),
        P("mp", "dp"),
        P(None, ("mp", "dp")),
        P(("mp", "dp")),
        P("mp", "dp"),
        P("dp", "mp"),
        P("dp", "mp"),
        P("mp", "dp"),
    )
    body = make_body(mesh.shape["dp"], mesh.shape["mp"])
    return jax.shard_map(body, mesh=mesh, in_specs=in_specs, out_specs=out_specs, check_vma=False)
```
